32 devices in a mesh: energy: 4 (over y, core), space: 8 (over z, x).
Axes of the slice: x: 2, y: 2, z: 4, core: 2. Of those that a mesh axis runs over, the one named last changes fastest.
Arguments:
- green_blocks: float32 [4, 16, 2, 1024, 1024], P('energy', 'space'), may hold values from -0.078125 to 0.078125
- injection: float32 [4, 16, 2, 1024], P('energy', 'space'), may hold values from 0.3 to 27
- mesh_state_choice: int32 [256, 64, 128], P('space'), may hold values from 0 to 1023
- regions: int32 [256, 64, 128], P('space', 'energy'), may hold values from 0 to 2
- dopant_charge_field: float32 [256, 64, 128], P('space', 'energy'), may hold values from -18 to 32
- earlier_voltage: float32 [256, 64, 128], P('space'), may hold values from -3 to 3
Outputs:
- potential: float32 [256, 64, 128], P('space')
The draws below stay inside these ranges and needn't reach their ends.
All inputs are finite; a program needn't handle non-finite values. Where the reference program divides by a largest or mean magnitude, that divisor is 1e-20 or more.
Results may differ from the reference program's by a relative error of at most 0.00007.
Values sent between devices are 32-bit elements; how exact they have to be, the bound alone decides.
No kernel may reach another device: no remote copies, remote signals or barrier semaphores. Data moves between devices by JAX's collectives and lax.ppermute only.
A program may use at most 320 MiB of HBM per device.

```python
import jax
import jax.numpy as jnp
from jax import lax

ATOMIC_STATES = 1024
PL = 16
CROSS_HEIGHT = 64
CROSS_WIDTH = 128
SWEEPS = 4
ENERGIES = 4
SLAB_TOTAL = 16
WIRE_LAYER_TOTAL = 256


def draw_injection(key, part):
    key = jax.random.fold_in(key, 7)
    spectral_step_number = (jnp.arange(ENERGIES, dtype=jnp.float32) / max(ENERGIES - 1, 1))[:, None, None, None]
    species_sign = jnp.arange(2, dtype=jnp.float32)[None, None, :, None]
    levels = jnp.exp(jax.random.uniform(key, (ENERGIES, SLAB_TOTAL, 2, ATOMIC_STATES), jnp.float32, -1.204, 1.0986))
    factor = 3.0
    thermal_argument = spectral_step_number * (1.0 - species_sign) + (1.0 - spectral_step_number) * species_sign
    return (levels * factor ** thermal_argument).astype(jnp.float32)


def draw_dopant_charge_field(key, part):
    key = jax.random.fold_in(key, 13)
    plane = (jnp.arange(WIRE_LAYER_TOTAL, dtype=jnp.float32) / WIRE_LAYER_TOTAL)[:, None, None]
    across = (jnp.arange(CROSS_HEIGHT, dtype=jnp.float32) / CROSS_HEIGHT)[None, :, None]
    rough = jnp.clip(jax.random.normal(key, (WIRE_LAYER_TOTAL, CROSS_HEIGHT, CROSS_WIDTH), jnp.float32), -4.0, 4.0)
    ramp = (1.0 + 2.0 * plane) * (1.0 + 2.0 * across)
    return (0.5 * rough * ramp).astype(jnp.float32)


def touch_ends(drawn, rng, least, high):
    longest = drawn.shape.index(max(drawn.shape))
    spots = []
    for shift in (0, 1):
        where = [jax.random.randint(jax.random.fold_in(rng, axis), (), 0, length) for axis, length in enumerate(drawn.shape)]
        where[longest] = (where[longest] + shift) % drawn.shape[longest]
        spots.append(tuple(where))
    return drawn.at[spots[0]].set(least).at[spots[1]].set(high)


def block_levels(key, extent, cuts, least, top_value):
    def one(axis_at, blocks):
        draws = jax.random.uniform(jax.random.fold_in(jax.random.fold_in(key, 6), axis_at), (blocks,), jnp.float32, least / len(cuts), top_value / len(cuts))
        return jnp.repeat(jnp.exp(draws), extent[axis_at] // blocks).reshape((-1,) + (1,) * (len(extent) - axis_at - 1))

    gain = one(*cuts[0])
    for cut in cuts[1:]:
        gain = gain * one(*cut)
    return gain


def bell_draw(stream_key, dims, width, limit, cuts=(), kind=jnp.bfloat16):
    loudness = block_levels(stream_key, dims, cuts, -0.22, 0.18) if cuts else 1.0
    entries = jax.random.normal(stream_key, dims, jnp.float32) * width * loudness
    return jnp.minimum(jnp.maximum(entries, -limit), limit).astype(kind)


def setup_inputs(seed: int = 0) -> dict:
    arg_keys = jax.random.split(jax.random.key(seed), 7)
    return {
        "green_blocks": bell_draw(arg_keys[0], (ENERGIES, SLAB_TOTAL, 2, ATOMIC_STATES, ATOMIC_STATES), 0.014, 0.078125, ((0, 4), (1, 8)), jnp.float32),
        "injection": draw_injection(jax.random.fold_in(arg_keys[6], 71), 0),
        "mesh_state_choice": touch_ends(jax.random.randint(arg_keys[2], (WIRE_LAYER_TOTAL, CROSS_HEIGHT, CROSS_WIDTH), 0, ATOMIC_STATES), jax.random.fold_in(arg_keys[2], 1), 0, ATOMIC_STATES - 1).astype(jnp.int32),
        "regions": touch_ends(jax.random.randint(arg_keys[3], (WIRE_LAYER_TOTAL, CROSS_HEIGHT, CROSS_WIDTH), 0, 3), jax.random.fold_in(arg_keys[3], 1), 0, 2).astype(jnp.int32),
        "dopant_charge_field": draw_dopant_charge_field(jax.random.fold_in(arg_keys[6], 71), 0),
        "earlier_voltage": bell_draw(arg_keys[5], (WIRE_LAYER_TOTAL, CROSS_HEIGHT, CROSS_WIDTH), 0.5, 3.0, ((0, 8),), jnp.float32),
    }


def permittivity(regions):
    return jnp.where(regions == 0, 1.0, jnp.where(regions == 1, 0.33, 1.7)).astype(jnp.float32)


def smoothed_voxels(haloed_voltage, dielectric_mesh, dopant_charge_field, electrons, hole_density, old_field):
    center = haloed_voltage[1:-1, 1:-1, :]
    along_z = jnp.pad(center, ((0, 0), (0, 0), (1, 1)))
    neighbours = haloed_voltage[2:, 1:-1, :] + haloed_voltage[:-2, 1:-1, :]
    neighbours = neighbours + haloed_voltage[1:-1, 2:, :] + haloed_voltage[1:-1, :-2, :]
    neighbours = neighbours + along_z[:, :, 2:] + along_z[:, :, :-2]
    raised = jnp.exp(center - old_field)
    lowered = jnp.exp(old_field - center)
    mismatch = dielectric_mesh * (6.0 * center - neighbours) - (dopant_charge_field + hole_density * lowered - electrons * raised)
    jacobian = 6.0 * dielectric_mesh + electrons * raised + hole_density * lowered
    return center - mismatch / jacobian


def slab_terms(green_slab, inject_slab):
    squared = green_slab[:, 0] * green_slab[:, 0] + green_slab[:, 1] * green_slab[:, 1]
    return jnp.einsum('eij,epj->pi', squared, inject_slab, precision=lax.Precision.HIGHEST)


def reference(green_blocks, injection, mesh_state_choice, regions, dopant_charge_field, earlier_voltage):
    state_occupation = lax.map(lambda slab_index: slab_terms(green_blocks[:, slab_index], injection[:, slab_index]),
                              jnp.arange(SLAB_TOTAL, dtype=jnp.int32))
    species_occupations = jnp.transpose(state_occupation, (1, 0, 2)).reshape(2, SLAB_TOTAL * ATOMIC_STATES)
    slab_of = (jnp.arange(WIRE_LAYER_TOTAL, dtype=jnp.int32) // PL)[:, None, None]
    linear_offset = (slab_of * ATOMIC_STATES + mesh_state_choice).reshape(-1).astype(jnp.int32)
    electron_mesh_charge = jnp.take(species_occupations, linear_offset, axis=1).reshape(2, WIRE_LAYER_TOTAL, CROSS_HEIGHT, CROSS_WIDTH)
    dielectric_mesh = permittivity(regions)
    electrostatic_sweep = earlier_voltage
    for sweep_step in range(SWEEPS):
        haloed_voltage = jnp.pad(electrostatic_sweep, ((1, 1), (1, 1), (0, 0)))
        electrostatic_sweep = smoothed_voxels(haloed_voltage, dielectric_mesh, dopant_charge_field, electron_mesh_charge[0], electron_mesh_charge[1], earlier_voltage)
    change = electrostatic_sweep - earlier_voltage
    largest = jnp.max(jnp.abs(change))
    return earlier_voltage + change / (1.0 + largest)
```

```python
import functools

import jax
import jax.numpy as jnp
from jax import lax
from jax.experimental import pallas as pl
from jax.experimental.pallas import tpu as pltpu
from jax.sharding import PartitionSpec as P

PL = 16
SWEEPS = 4
HALO = 4
PAD = 8
LANES = 128
SUB = 8
MIB = 1 << 20


def merge(parts, width):
    lane = lax.broadcasted_iota(jnp.int32, (SUB, LANES), 1)
    while len(parts) > 1:
        low = (lane & width) == 0
        merged = []
        for a, b in zip(parts[::2], parts[1::2]):
            merged.append(jnp.where(low, a, b) + pltpu.roll(jnp.where(low, b, a), width, 1))
        parts = merged
        width *= 2
    return parts[0]


def table_kernel(green_ref, inject_ref, out_ref, part_ref):
    rows = green_ref.shape[1]
    columns = green_ref.shape[2]
    groups = rows // SUB
    block = pl.program_id(1)
    chunks = columns // LANES
    weights = [
        [
            jnp.broadcast_to(inject_ref[c : c + 1, k * LANES : (k + 1) * LANES], (SUB, LANES))
            for k in range(chunks)
        ]
        for c in range(2)
    ]
    sums = [[], []]
    for g in range(groups):
        total = [None, None]
        for k in range(chunks):
            cols = slice(k * LANES, (k + 1) * LANES)
            re = green_ref[0, g * SUB : (g + 1) * SUB, cols]
            im = green_ref[1, g * SUB : (g + 1) * SUB, cols]
            squared = re * re + im * im
            for c in range(2):
                term = squared * weights[c][k]
                total[c] = term if total[c] is None else total[c] + term
        for c in range(2):
            sums[c].append(total[c])
    for c in range(2):
        part_ref[c, block] = merge(sums[c], 1)

    @pl.when(block == pl.num_programs(1) - 1)
    def _():
        count = part_ref.shape[1]
        for c in range(2):
            out_ref[c] = merge([part_ref[c, b] for b in range(count)], groups)


def orbital_table(green, inject):
    slabs, _, states, _ = green.shape
    rows = 128
    return pl.pallas_call(
        table_kernel,
        grid=(slabs, states // rows),
        in_specs=[
            pl.BlockSpec((None, 2, rows, states), lambda s, b: (s, 0, b, 0)),
            pl.BlockSpec((None, 2, states), lambda s, b: (s, 0, 0)),
        ],
        out_specs=pl.BlockSpec((None, 2, SUB, LANES), lambda s, b: (s, 0, 0, 0)),
        out_shape=jax.ShapeDtypeStruct((slabs, 2, SUB, LANES), jnp.float32),
        scratch_shapes=[pltpu.VMEM((2, states // rows, SUB, LANES), jnp.float32)],
        compiler_params=pltpu.CompilerParams(vmem_limit_bytes=32 * MIB),
        name="table",
    )(green, inject)


def lookup(tables, choice):
    lane = choice >> 3
    group = choice & (SUB - 1)
    bits = [(group & (1 << b)) != 0 for b in range(3)]
    out = []
    for table in tables:
        found = [jnp.take_along_axis(t, lane, axis=1, mode="promise_in_bounds") for t in table]
        for bit in bits:
            found = [jnp.where(bit, found[2 * k + 1], found[2 * k]) for k in range(len(found) // 2)]
        out.append(found[0])
    return out


def permittivity(regions):
    return jnp.where(regions == 0, 1.0, jnp.where(regions == 1, 0.33, 1.7)).astype(jnp.float32)


def sweep_kernel(
    place_ref, tables_ref, beside1_ref, beside2_ref,
    mesh_ref, old_ref, regions_ref, dopant_ref,
    rows1_ref, rows2_ref, planes1_ref, planes2_ref,
    change_ref, most_ref,
    mesh_s, before_s, permit_s, dopant_s, electron_s, hole_s, now_s, next_s,
):
    e, s, ne, ns = (place_ref[k] for k in range(4))
    odd_e, odd_s = (e & 1) == 1, (s & 1) == 1
    planes, own, _ = regions_ref.shape
    slabs = tables_ref.shape[0]
    span = own + 2 * HALO
    row0 = e * own
    first, last = PAD, PAD + span
    full_rows = mesh_ref.shape[1]

    up_in, down_in = e > 0, e < ne - 1
    mid = slice(PAD + HALO, PAD + HALO + own)
    up = slice(PAD, PAD + HALO)
    down = slice(PAD + HALO + own, PAD + span)
    body = slice(HALO, HALO + planes)
    up_from = pl.multiple_of(jnp.maximum(row0 - SUB, 0), SUB)
    down_from = pl.multiple_of(jnp.minimum(row0 + own, full_rows - SUB), SUB)

    def lay(p, _):
        q = p + HALO
        mesh_s[q, mid] = mesh_ref[p, pl.ds(row0, own)]
        mesh_s[q, up] = mesh_ref[p, pl.ds(up_from, SUB)][SUB - HALO :]
        mesh_s[q, down] = mesh_ref[p, pl.ds(down_from, SUB)][:HALO]
        before_s[q, mid] = old_ref[p, pl.ds(row0, own)]
        before_s[q, up] = jnp.where(up_in, old_ref[p, pl.ds(up_from, SUB)][SUB - HALO :], 0.0)
        before_s[q, down] = jnp.where(down_in, old_ref[p, pl.ds(down_from, SUB)][:HALO], 0.0)
        permit_s[q, mid] = permittivity(regions_ref[p])
        dopant_s[q, mid] = dopant_ref[p]
        permit_s[q, up] = jnp.where(odd_e, rows1_ref[0, p], rows2_ref[0, p])
        permit_s[q, down] = jnp.where(odd_e, rows2_ref[0, p], rows1_ref[0, p])
        dopant_s[q, up] = jnp.where(odd_e, rows1_ref[1, p], rows2_ref[1, p])
        dopant_s[q, down] = jnp.where(odd_e, rows2_ref[1, p], rows1_ref[1, p])
        return _

    lax.fori_loop(0, planes, lay, None)
    whole = slice(PAD, PAD + span)
    for k in range(HALO):
        for q, a, b in ((k, planes1_ref, planes2_ref), (HALO + planes + k, planes2_ref, planes1_ref)):
            mesh_s[q, whole] = jnp.where(odd_s, a[0, k], b[0, k]).astype(jnp.int32)
            before_s[q, whole] = jnp.where(odd_s, a[1, k], b[1, k])
            permit_s[q, whole] = jnp.where(odd_s, a[2, k], b[2, k])
            dopant_s[q, whole] = jnp.where(odd_s, a[3, k], b[3, k])

    def table_of(slab_value):
        return [
            [jnp.broadcast_to(slab_value[c, g : g + 1], (SUB, LANES)) for g in range(SUB)]
            for c in range(2)
        ]

    def densities(q, tables):
        for r in range(PAD, PAD + span, SUB):
            found = lookup(tables, mesh_s[q, r : r + SUB])
            electron_s[q, r : r + SUB] = found[0]
            hole_s[q, r : r + SUB] = found[1]

    low_table = table_of(jnp.where(odd_s, beside1_ref[...], beside2_ref[...]))
    for q in range(1, HALO):
        densities(q, low_table)
    for slab in range(slabs):
        table = table_of(tables_ref[slab])

        def one(p, _, table=table):
            densities(p, table)
            return _

        lax.fori_loop(HALO + slab * PL, HALO + (slab + 1) * PL, one, None)
    high_table = table_of(jnp.where(odd_s, beside2_ref[...], beside1_ref[...]))
    for q in range(HALO + planes, HALO + planes + HALO - 1):
        densities(q, high_table)

    lane = lax.broadcasted_iota(jnp.int32, (SUB, LANES), 1)
    not_first, not_last = lane > 0, lane < LANES - 1
    row = lax.broadcasted_iota(jnp.int32, (SUB, LANES), 0)
    for buffer in (now_s, next_s):
        for q in (0, 1, 2, 3, planes + 4, planes + 5, planes + 6, planes + 7):
            buffer[q] = jnp.zeros(buffer.shape[1:], jnp.float32)
    low_plane = jnp.where(s > 0, 0, HALO)
    high_plane = jnp.where(s < ns - 1, planes + 2 * HALO, planes + HALO)
    most_ref[...] = jnp.zeros(most_ref.shape, jnp.float32)
    source = before_s
    for sweep in range(SWEEPS):
        final = sweep == SWEEPS - 1
        target = next_s if source is now_s else now_s
        starts = range(PAD + HALO, PAD + HALO + own, SUB) if final else range(PAD, PAD + span, SUB)

        def step(q, most, sweep=sweep, source=source, target=target, starts=starts, final=final):
            for r in starts:
                rows = slice(r, r + SUB)
                center = source[q, rows]
                neighbours = source[q + 1, rows] + source[q - 1, rows]
                neighbours = neighbours + source[q, r + 1 : r + 1 + SUB] + source[q, r - 1 : r - 1 + SUB]
                after = jnp.where(not_last, pltpu.roll(center, LANES - 1, 1), 0.0)
                ahead = jnp.where(not_first, pltpu.roll(center, 1, 1), 0.0)
                neighbours = neighbours + after + ahead
                permit = permit_s[q, rows]
                electrons = electron_s[q, rows]
                holes = hole_s[q, rows]
                if sweep:
                    moved = center - before_s[q, rows]
                    electrons = electrons * jnp.exp(moved)
                    holes = holes * jnp.exp(-moved)
                mismatch = permit * (6.0 * center - neighbours) - (dopant_s[q, rows] + holes - electrons)
                jacobian = 6.0 * permit + electrons + holes
                fresh = center - mismatch / jacobian
                if final:
                    change = fresh - before_s[q, rows]
                    change_ref[q - HALO, r - PAD - HALO : r - PAD - HALO + SUB] = change
                    most = jnp.maximum(most, jnp.abs(change))
                else:
                    if r == PAD:
                        fresh = jnp.where((row >= HALO) | up_in, fresh, 0.0)
                    elif r == PAD + span - SUB:
                        fresh = jnp.where((row < HALO) | down_in, fresh, 0.0)
                    target[q, rows] = fresh
            return most

        begin = jnp.maximum(low_plane, 1 + sweep)
        end = jnp.minimum(high_plane, planes + 2 * HALO - 1 - sweep)
        most = lax.fori_loop(begin, end, step, jnp.zeros((SUB, LANES), jnp.float32))
        if final:
            most_ref[...] = jnp.max(most, axis=0, keepdims=True)
        source = target


def swept(place, tables, beside, mesh, old, regions, dopant, rows, edge_planes):
    planes, own, lanes = regions.shape
    deep = (planes + 2 * HALO, own + 2 * HALO + 2 * PAD, lanes)
    vmem = pl.BlockSpec(memory_space=pltpu.VMEM)
    return pl.pallas_call(
        sweep_kernel,
        in_specs=[pl.BlockSpec(memory_space=pltpu.SMEM)] + [vmem] * 11,
        out_specs=[vmem, vmem],
        out_shape=[
            jax.ShapeDtypeStruct(regions.shape, jnp.float32),
            jax.ShapeDtypeStruct((1, lanes), jnp.float32),
        ],
        scratch_shapes=[pltpu.VMEM(deep, jnp.int32)] + [pltpu.VMEM(deep, jnp.float32)] * 7,
        compiler_params=pltpu.CompilerParams(vmem_limit_bytes=40 * MIB),
        name="sweeps",
    )(place, tables, *beside, mesh, old, regions, dopant, *rows, *edge_planes)


def settle_kernel(place_ref, most_ref, old_ref, *rest):
    parts, out_ref = rest[:-1], rest[-1]
    e = place_ref[0]
    own = parts[0].shape[1]
    largest = jnp.max(most_ref[...])
    for k, part in enumerate(parts):
        rows = pl.ds(pl.multiple_of((e ^ k) * own, SUB), own)
        out_ref[:, rows] = old_ref[:, rows] + part[...] / (1.0 + largest)


def settled(place, most, old, parts):
    vmem = pl.BlockSpec(memory_space=pltpu.VMEM)
    return pl.pallas_call(
        settle_kernel,
        in_specs=[pl.BlockSpec(memory_space=pltpu.SMEM)] + [vmem] * (2 + len(parts)),
        out_specs=vmem,
        out_shape=jax.ShapeDtypeStruct(old.shape, jnp.float32),
        compiler_params=pltpu.CompilerParams(vmem_limit_bytes=32 * MIB),
        name="settle",
    )(place, most, old, *parts)


def pairs(axis, odd_first):
    count = lax.axis_size(axis)
    out = []
    for low in range(1 if odd_first else 0, count - 1, 2):
        out += [(low, low + 1), (low + 1, low)]
    return out


def toggled(x, axis, mask):
    return lax.ppermute(x, axis, [(i, i ^ mask) for i in range(lax.axis_size(axis))])


def on_device(green_blocks, injection, mesh_state_choice, regions, dopant_charge_field, earlier_voltage):
    ne, ns = lax.axis_size("energy"), lax.axis_size("space")
    e, s = lax.axis_index("energy"), lax.axis_index("space")
    planes, own, lanes = regions.shape
    odd_e, odd_s = e & 1, s & 1
    place = jnp.stack([e, s, jnp.int32(ne), jnp.int32(ns)]).astype(jnp.int32)

    permit = permittivity(regions)
    fields = jnp.stack([permit, dopant_charge_field])
    rows = []
    for odd_first in (False, True):
        at_top = odd_e if not odd_first else 1 - odd_e
        edge = lax.dynamic_slice_in_dim(fields, (1 - at_top) * (own - HALO), HALO, 2)
        rows.append(lax.ppermute(edge, "energy", pairs("energy", odd_first)))
    above = jnp.where(odd_e == 1, rows[0], rows[1])
    below = jnp.where(odd_e == 1, rows[1], rows[0])
    edge_planes = []
    for odd_first in (False, True):
        at_low = odd_s if not odd_first else 1 - odd_s
        start = (1 - at_low) * (planes - HALO)
        cut = functools.partial(lax.dynamic_slice_in_dim, start_index=start, slice_size=HALO)
        taken = []
        for field in (mesh_state_choice, earlier_voltage):
            tall = jnp.pad(cut(field, axis=0), ((0, 0), (HALO, HALO), (0, 0)))
            taken.append(lax.dynamic_slice_in_dim(tall, e * own, own + 2 * HALO, 1).astype(jnp.float32))
        stacked = jnp.stack(taken)
        both = jnp.concatenate([cut(above, axis=1), cut(fields, axis=1), cut(below, axis=1)], axis=2)
        edge_planes.append(
            lax.ppermute(jnp.concatenate([stacked, both]), "space", pairs("space", odd_first))
        )

    tables = orbital_table(green_blocks[0], injection[0])
    terms = [tables] + [toggled(tables, "energy", k) for k in range(1, ne)]
    while len(terms) > 1:
        terms = [terms[2 * k] + terms[2 * k + 1] for k in range(len(terms) // 2)]
    tables = terms[0]
    beside = []
    for odd_first in (False, True):
        at_low = odd_s if not odd_first else 1 - odd_s
        edge = jnp.where(at_low == 1, tables[0], tables[-1])
        beside.append(lax.ppermute(edge, "space", pairs("space", odd_first)))

    change, most = swept(
        place, tables, beside, mesh_state_choice, earlier_voltage, regions, dopant_charge_field,
        rows, edge_planes,
    )
    parts = [change] + [toggled(change, "energy", k) for k in range(1, ne)]
    spread = jnp.broadcast_to(most[None], (ne * ns, 1, lanes))
    most = lax.all_to_all(spread, ("energy", "space"), 0, 0)
    return settled(place, most.reshape(ne * ns, lanes), earlier_voltage, parts)


def solution(mesh):
    placed = (
        P("energy", "space", None, None, None),
        P("energy", "space", None, None),
        P("space", None, None),
        P("space", "energy", None),
        P("space", "energy", None),
        P("space", None, None),
    )
    return jax.shard_map(
        on_device, mesh=mesh, in_specs=placed, out_specs=P("space", None, None), check_vma=False
    )
```

```python
import functools

import jax
import jax.numpy as jnp
from jax import lax
from jax.experimental import pallas as pl
from jax.experimental.pallas import tpu as pltpu
from jax.sharding import PartitionSpec as P

PL = 16
SWEEPS = 4
HALO = 4
PAD = 8
LANES = 128
SUB = 8
MIB = 1 << 20
BLOCK = 8
LOOK = 4
LAY = 4
SETTLE = 4
EDGE_COST = 10 * MIB
TABLE_COST = 10 * MIB
LAY_COST = 3 * MIB
LATER = pl.ANY
PAIRS = 16


def merge(parts, width):
    lane = lax.broadcasted_iota(jnp.int32, (SUB, LANES), 1)
    while len(parts) > 1:
        low = (lane & width) == 0
        merged = []
        for a, b in zip(parts[::2], parts[1::2]):
            merged.append(jnp.where(low, a, b) + pltpu.roll(jnp.where(low, b, a), width, 1))
        parts = merged
        width *= 2
    return parts[0]


def table_kernel(green_ref, inject_ref, out_ref, part_ref):
    slabs, _, states, columns = green_ref.shape
    chunks = columns // LANES
    groups = states // SUB
    for slab in range(slabs):
        weights = [
            [
                jnp.broadcast_to(inject_ref[slab, c : c + 1, k * LANES : (k + 1) * LANES], (SUB, LANES))
                for k in range(chunks)
            ]
            for c in range(2)
        ]

        def some_groups(i, _, slab=slab, weights=weights):
            for pair in range(PAIRS):
                sums = [[], []]
                for g in range(2):
                    rows = pl.ds(pl.multiple_of((i * (2 * PAIRS) + 2 * pair + g) * SUB, SUB), SUB)
                    total = [None, None]
                    for k in range(chunks):
                        cols = slice(k * LANES, (k + 1) * LANES)
                        re = green_ref[slab, 0, rows, cols]
                        im = green_ref[slab, 1, rows, cols]
                        squared = re * re + im * im
                        for c in range(2):
                            term = squared * weights[c][k]
                            total[c] = term if total[c] is None else total[c] + term
                    for c in range(2):
                        sums[c].append(total[c])
                for c in range(2):
                    part_ref[slab, c, i * PAIRS + pair] = merge(sums[c], 1)
            return _

        lax.fori_loop(0, groups // (2 * PAIRS), some_groups, None)
    lane = lax.broadcasted_iota(jnp.int32, (SUB, LANES), 1)
    count, width = groups // 2, 2
    while count > 1:
        low = (lane & width) == 0
        count //= 2
        for slab in range(slabs):
            for c in range(2):
                for k in range(count):
                    a, b = part_ref[slab, c, 2 * k], part_ref[slab, c, 2 * k + 1]
                    both = jnp.where(low, a, b) + pltpu.roll(jnp.where(low, b, a), width, 1)
                    if count > 1:
                        part_ref[slab, c, k] = both
                    else:
                        out_ref[slab, c] = both
        width *= 2


def orbital_table(green, inject):
    slabs, _, states, _ = green.shape
    vmem = pl.BlockSpec(memory_space=pltpu.VMEM)
    return pl.pallas_call(
        table_kernel,
        in_specs=[vmem, vmem],
        out_specs=vmem,
        out_shape=jax.ShapeDtypeStruct((slabs, 2, SUB, LANES), jnp.float32),
        scratch_shapes=[pltpu.VMEM((slabs, 2, states // SUB // 2, SUB, LANES), jnp.float32)],
        compiler_params=pltpu.CompilerParams(vmem_limit_bytes=20 * MIB),
        cost_estimate=pl.CostEstimate(flops=0, bytes_accessed=TABLE_COST, transcendentals=0),
        name="table",
    )(green, inject)


def lookup(tables, choice):
    lane = choice >> 3
    group = choice & (SUB - 1)
    bits = [(group & (1 << b)) != 0 for b in range(3)]
    out = []
    for table in tables:
        found = [jnp.take_along_axis(t, lane, axis=1, mode="promise_in_bounds") for t in table]
        for bit in bits:
            found = [jnp.where(bit, found[2 * k + 1], found[2 * k]) for k in range(len(found) // 2)]
        out.append(found[0])
    return out


def permittivity(regions):
    return jnp.where(regions == 0, 1.0, jnp.where(regions == 1, 0.33, 1.7)).astype(jnp.float32)


def grouped(count, size, step, carry):
    odd = count % size
    if odd:
        carry = step(0, odd, carry)
    return lax.fori_loop(0, count // size, lambda i, c: step(odd + i * size, size, c), carry)


def around(center, below, above, left, right):
    lane = lax.broadcasted_iota(jnp.int32, (SUB, LANES), 1)
    after = jnp.where(lane < LANES - 1, pltpu.roll(center, LANES - 1, 1), 0.0)
    ahead = jnp.where(lane > 0, pltpu.roll(center, 1, 1), 0.0)
    return above + below + right + left + after + ahead


def position():
    return lax.axis_index("energy"), lax.axis_index("space"), lax.axis_size("energy"), lax.axis_size("space")


def edge_rows_kernel(regions_ref, dopant_ref, green_ref, inject_ref, mesh_ref, old_ref, first_ref, second_ref):
    odd = (lax.axis_index("energy") & 1) == 1
    planes, own, _ = regions_ref.shape
    top, bottom = slice(0, HALO), slice(own - HALO, own)

    def pack(first, count, _):
        for k in range(count):
            p = first + k
            permit = permittivity(regions_ref[p])
            dopant = dopant_ref[p]
            for field, values in ((0, permit), (1, dopant)):
                first_ref[field, p] = jnp.where(odd, values[top], values[bottom])
                second_ref[field, p] = jnp.where(odd, values[bottom], values[top])
        return _

    grouped(planes, LAY, pack, None)


def edge_rows(regions, dopant, *later):
    planes, _, lanes = regions.shape
    vmem = pl.BlockSpec(memory_space=pltpu.VMEM)
    return pl.pallas_call(
        edge_rows_kernel,
        in_specs=[vmem] * 2 + [pl.BlockSpec(memory_space=LATER)] * len(later),
        out_specs=[vmem] * 2,
        out_shape=[jax.ShapeDtypeStruct((2, planes, HALO, lanes), jnp.float32)] * 2,
        compiler_params=pltpu.CompilerParams(vmem_limit_bytes=4 * MIB),
        cost_estimate=pl.CostEstimate(flops=0, bytes_accessed=EDGE_COST, transcendentals=0),
        name="edge_rows",
    )(regions, dopant, *(pltpu.with_memory_space_constraint(x, pltpu.HBM) for x in later))


def edge_planes_kernel(mesh_ref, old_ref, regions_ref, dopant_ref, rows1_ref, rows2_ref, first_ref, second_ref):
    e, s, ne, _ = position()
    odd_e, odd_s = (e & 1) == 1, (s & 1) == 1
    planes, own, _ = regions_ref.shape
    row0 = pl.multiple_of(e * own, SUB)
    full_rows = mesh_ref.shape[1]
    up_from = pl.multiple_of(jnp.maximum(row0 - SUB, 0), SUB)
    down_from = pl.multiple_of(jnp.minimum(row0 + own, full_rows - SUB), SUB)
    up, mid, down = slice(0, HALO), slice(HALO, HALO + own), slice(HALO + own, own + 2 * HALO)
    near = HALO - 1
    for out_ref, at_low in ((first_ref, odd_s), (second_ref, jnp.logical_not(odd_s))):
        for k in range(HALO):
            p = jnp.where(at_low, k, planes - HALO + k)
            out_ref[3 * near + k, up] = jnp.where(e > 0, old_ref[p, pl.ds(up_from, SUB)][SUB - HALO :], 0.0)
            out_ref[3 * near + k, mid] = old_ref[p, pl.ds(row0, own)]
            out_ref[3 * near + k, down] = jnp.where(e < ne - 1, old_ref[p, pl.ds(down_from, SUB)][:HALO], 0.0)
        for k in range(near):
            p = jnp.where(at_low, k, planes - near + k)
            out_ref[k, up] = mesh_ref[p, pl.ds(up_from, SUB)][SUB - HALO :].astype(jnp.float32)
            out_ref[k, mid] = mesh_ref[p, pl.ds(row0, own)].astype(jnp.float32)
            out_ref[k, down] = mesh_ref[p, pl.ds(down_from, SUB)][:HALO].astype(jnp.float32)
            out_ref[near + k, mid] = permittivity(regions_ref[p])
            out_ref[2 * near + k, mid] = dopant_ref[p]
            for field in range(2):
                at = (1 + field) * near + k
                out_ref[at, up] = jnp.where(odd_e, rows1_ref[field, p], rows2_ref[field, p])
                out_ref[at, down] = jnp.where(odd_e, rows2_ref[field, p], rows1_ref[field, p])


def edge_planes(mesh, old, regions, dopant, rows):
    _, own, lanes = regions.shape
    vmem = pl.BlockSpec(memory_space=pltpu.VMEM)
    shape = (3 * (HALO - 1) + HALO, own + 2 * HALO, lanes)
    return pl.pallas_call(
        edge_planes_kernel,
        in_specs=[vmem] * 6,
        out_specs=[vmem] * 2,
        out_shape=[jax.ShapeDtypeStruct(shape, jnp.float32)] * 2,
        compiler_params=pltpu.CompilerParams(vmem_limit_bytes=8 * MIB),
        cost_estimate=pl.CostEstimate(flops=0, bytes_accessed=EDGE_COST, transcendentals=0),
        name="edge_planes",
    )(mesh, old, regions, dopant, *rows)


def lay_kernel(
    mesh_ref, old_ref, regions_ref, dopant_ref, rows1_ref, rows2_ref, planes1_ref, planes2_ref,
    mesh_x, before_x, permit_x, dopant_x, first_x,
):
    e, s, ne, ns = position()
    odd_e, odd_s = (e & 1) == 1, (s & 1) == 1
    planes, own, _ = regions_ref.shape
    span = own + 2 * HALO
    row0 = pl.multiple_of(e * own, SUB)
    full_rows = mesh_ref.shape[1]
    up_in, down_in = e > 0, e < ne - 1
    up, mid, down = slice(0, HALO), slice(HALO, HALO + own), slice(HALO + own, span)
    up_b, mid_b, down_b = (slice(PAD + x.start, PAD + x.stop) for x in (up, mid, down))
    up_from = pl.multiple_of(jnp.maximum(row0 - SUB, 0), SUB)
    down_from = pl.multiple_of(jnp.minimum(row0 + own, full_rows - SUB), SUB)

    def lay(first, count, _):
        for k in range(count):
            p = first + k
            q = p + HALO
            mesh_x[q, mid] = mesh_ref[p, pl.ds(row0, own)]
            mesh_x[q, up] = mesh_ref[p, pl.ds(up_from, SUB)][SUB - HALO :]
            mesh_x[q, down] = mesh_ref[p, pl.ds(down_from, SUB)][:HALO]
            before_x[q, mid_b] = old_ref[p, pl.ds(row0, own)]
            before_x[q, up_b] = jnp.where(up_in, old_ref[p, pl.ds(up_from, SUB)][SUB - HALO :], 0.0)
            before_x[q, down_b] = jnp.where(down_in, old_ref[p, pl.ds(down_from, SUB)][:HALO], 0.0)
            permit_x[q, mid] = permittivity(regions_ref[p])
            dopant_x[q, mid] = dopant_ref[p]
            permit_x[q, up] = jnp.where(odd_e, rows1_ref[0, p], rows2_ref[0, p])
            permit_x[q, down] = jnp.where(odd_e, rows2_ref[0, p], rows1_ref[0, p])
            dopant_x[q, up] = jnp.where(odd_e, rows1_ref[1, p], rows2_ref[1, p])
            dopant_x[q, down] = jnp.where(odd_e, rows2_ref[1, p], rows1_ref[1, p])
        return _

    grouped(planes, LAY, lay, None)
    whole_b = slice(PAD, PAD + span)
    near = HALO - 1
    for low in (True, False):
        a, b = (planes1_ref, planes2_ref) if low else (planes2_ref, planes1_ref)
        for k in range(near):
            q = 1 + k if low else HALO + planes + k
            mesh_x[q] = jnp.where(odd_s, a[k], b[k]).astype(jnp.int32)
            permit_x[q] = jnp.where(odd_s, a[near + k], b[near + k])
            dopant_x[q] = jnp.where(odd_s, a[2 * near + k], b[2 * near + k])
        for k in range(HALO):
            q = k if low else HALO + planes + k
            before_x[q, whole_b] = jnp.where(odd_s, a[3 * near + k], b[3 * near + k])

    def terms(first, count, _):
        for r in range(0, span, SUB):
            held = [before_x[1 + first + k, PAD + r : PAD + r + SUB] for k in range(-1, count + 1)]
            for k in range(count):
                q = 1 + first + k
                neighbours = around(
                    held[k + 1], held[k], held[k + 2],
                    before_x[q, PAD + r - 1 : PAD + r - 1 + SUB], before_x[q, PAD + r + 1 : PAD + r + 1 + SUB],
                )
                rows = slice(r, r + SUB)
                first_x[q, rows] = permit_x[q, rows] * (6.0 * held[k + 1] - neighbours) - dopant_x[q, rows]
        return _

    grouped(planes + 2 * near, BLOCK, terms, None)


def laid(mesh, old, regions, dopant, rows, edge_planes):
    planes, own, lanes = regions.shape
    cells = (planes + 2 * HALO, own + 2 * HALO, lanes)
    padded = (cells[0], cells[1] + 2 * PAD, lanes)
    vmem = pl.BlockSpec(memory_space=pltpu.VMEM)
    f32 = jnp.float32
    return pl.pallas_call(
        lay_kernel,
        in_specs=[vmem] * 8,
        out_specs=[vmem] * 5,
        out_shape=[
            jax.ShapeDtypeStruct(shape, kind)
            for shape, kind in ((cells, jnp.int32), (padded, f32), (cells, f32), (cells, f32), (cells, f32))
        ],
        compiler_params=pltpu.CompilerParams(vmem_limit_bytes=16 * MIB),
        cost_estimate=pl.CostEstimate(flops=0, bytes_accessed=LAY_COST, transcendentals=0),
        name="lay",
    )(mesh, old, regions, dopant, *rows, *edge_planes)


def sweep_kernel(
    tables_ref, beside1_ref, beside2_ref, mesh_x, before_x, permit_x, dopant_x, first_x,
    change_ref, most_ref, electron_s, hole_s, now_s, next_s,
):
    e, s, ne, ns = position()
    odd_s = (s & 1) == 1
    planes, own, _ = change_ref.shape
    slabs = tables_ref.shape[0]
    span = own + 2 * HALO
    up_in, down_in = e > 0, e < ne - 1
    tops = range(0, span, SUB)
    row = lax.broadcasted_iota(jnp.int32, (SUB, LANES), 0)

    def table_of(slab_value):
        return [
            [jnp.broadcast_to(slab_value[c, g : g + 1], (SUB, LANES)) for g in range(SUB)]
            for c in range(2)
        ]

    def densities(q, tables):
        for r in tops:
            rows = slice(r, r + SUB)
            found = lookup(tables, mesh_x[q, rows])
            if r == tops[0]:
                found = [jnp.where((row >= HALO) | up_in, v, 1.0) for v in found]
            if r == tops[-1]:
                found = [jnp.where((row < HALO) | down_in, v, 1.0) for v in found]
            electrons, holes = found
            electron_s[q, rows] = electrons
            hole_s[q, rows] = holes
            mismatch = first_x[q, rows] + electrons - holes
            jacobian = 6.0 * permit_x[q, rows] + electrons + holes
            now_s[q, PAD + r : PAD + r + SUB] = before_x[q, PAD + r : PAD + r + SUB] - mismatch / jacobian

    for slab in range(slabs):
        table = table_of(tables_ref[slab])

        def some(first, count, _, table=table, slab=slab):
            for k in range(count):
                densities(HALO + slab * PL + first + k, table)
            return _

        grouped(PL, LOOK, some, None)
    low_table = table_of(jnp.where(s > 0, jnp.where(odd_s, beside1_ref[...], beside2_ref[...]), 1.0))
    for q in range(1, HALO):
        densities(q, low_table)
    high_table = table_of(jnp.where(s < ns - 1, jnp.where(odd_s, beside2_ref[...], beside1_ref[...]), 1.0))
    for q in range(HALO + planes, HALO + planes + HALO - 1):
        densities(q, high_table)

    source = now_s
    for sweep in range(1, SWEEPS):
        final = sweep == SWEEPS - 1
        target = next_s if source is now_s else now_s
        starts = range(HALO, HALO + own, SUB) if final else tops

        def step(first, count, most, sweep=sweep, source=source, target=target, starts=starts, final=final):
            for r in starts:
                rows = slice(r, r + SUB)
                at = PAD + r
                rows_b = slice(at, at + SUB)
                held = [source[1 + sweep + first + k, rows_b] for k in range(-1, count + 1)]
                for k in range(count):
                    q = 1 + sweep + first + k
                    center = held[k + 1]
                    neighbours = around(
                        center, held[k], held[k + 2],
                        source[q, at - 1 : at - 1 + SUB], source[q, at + 1 : at + 1 + SUB],
                    )
                    permit = permit_x[q, rows]
                    before = before_x[q, rows_b]
                    moved = center - before
                    electrons = electron_s[q, rows] * jnp.exp(moved)
                    holes = hole_s[q, rows] * jnp.exp(-moved)
                    mismatch = permit * (6.0 * center - neighbours) - (dopant_x[q, rows] + holes - electrons)
                    jacobian = 6.0 * permit + electrons + holes
                    fresh = center - mismatch / jacobian
                    if final:
                        change = fresh - before
                        change_ref[q - HALO, r - HALO : r - HALO + SUB] = change
                        most = jnp.maximum(most, jnp.abs(change))
                    else:
                        target[q, rows_b] = fresh
            return most

        most = grouped(planes + 2 * (SWEEPS - 1 - sweep), BLOCK, step, jnp.zeros((SUB, LANES), jnp.float32))
        if final:
            most_ref[...] = jnp.broadcast_to(jnp.max(most, axis=0, keepdims=True)[None], most_ref.shape)
        source = target


def swept(tables, beside, fields, own):
    cells, padded = fields[0].shape, fields[1].shape
    planes, lanes = cells[0] - 2 * HALO, cells[2]
    vmem = pl.BlockSpec(memory_space=pltpu.VMEM)
    f32 = jnp.float32
    return pl.pallas_call(
        sweep_kernel,
        in_specs=[vmem] * 8,
        out_specs=[vmem, vmem],
        out_shape=[
            jax.ShapeDtypeStruct((planes, own, lanes), f32),
            jax.ShapeDtypeStruct((lax.axis_size(("energy", "space")), 1, lanes), f32),
        ],
        scratch_shapes=[pltpu.VMEM(cells, f32)] * 2 + [pltpu.VMEM(padded, f32)] * 2,
        compiler_params=pltpu.CompilerParams(vmem_limit_bytes=24 * MIB),
        name="sweeps",
    )(tables, *beside, *fields)


def settle_kernel(most_ref, old_ref, *rest):
    parts, out_ref, result, sems = rest[:-3], rest[-3], rest[-2], rest[-1]
    e = lax.axis_index("energy")
    planes, own, _ = parts[0].shape
    scale = 1.0 / (1.0 + jnp.max(most_ref[...]))
    size = planes // SETTLE
    copies = []
    for b in range(SETTLE):
        at = slice(b * size, (b + 1) * size)
        for k, part in enumerate(parts):
            rows = pl.ds(pl.multiple_of((e ^ k) * own, SUB), own)
            result[at, rows] = old_ref[at, rows] + part[at] * scale
        copies.append(pltpu.make_async_copy(result.at[at], out_ref.at[at], sems.at[b]))
        copies[-1].start()
    for copy in copies:
        copy.wait()


def settled(most, old, parts):
    vmem = pl.BlockSpec(memory_space=pltpu.VMEM)
    return pl.pallas_call(
        settle_kernel,
        in_specs=[vmem] * (2 + len(parts)),
        out_specs=pl.BlockSpec(memory_space=pl.ANY),
        out_shape=jax.ShapeDtypeStruct(old.shape, jnp.float32),
        scratch_shapes=[pltpu.VMEM(old.shape, jnp.float32), pltpu.SemaphoreType.DMA((SETTLE,))],
        compiler_params=pltpu.CompilerParams(vmem_limit_bytes=16 * MIB),
        name="settle",
    )(most, old, *parts)


def pairs(axis, odd_first):
    count = lax.axis_size(axis)
    out = []
    for low in range(1 if odd_first else 0, count - 1, 2):
        out += [(low, low + 1), (low + 1, low)]
    return out


def toggled(x, axis, mask):
    return lax.ppermute(x, axis, [(i, i ^ mask) for i in range(lax.axis_size(axis))])


def on_device(green_blocks, injection, mesh_state_choice, regions, dopant_charge_field, earlier_voltage):
    ne, ns = lax.axis_size("energy"), lax.axis_size("space")
    odd_s = lax.axis_index("space") & 1
    _, own, lanes = regions.shape

    rows = [
        lax.ppermute(x, "energy", pairs("energy", odd_first))
        for x, odd_first in zip(edge_rows(regions, dopant_charge_field, green_blocks[0], injection[0], mesh_state_choice, earlier_voltage), (False, True))
    ]
    sent = edge_planes(mesh_state_choice, earlier_voltage, regions, dopant_charge_field, rows)
    beyond = [lax.ppermute(x, "space", pairs("space", odd)) for x, odd in zip(sent, (False, True))]

    inject, _ = lax.optimization_barrier((injection[0], sent))
    tables = orbital_table(green_blocks[0], inject)
    terms = [tables] + [toggled(tables, "energy", k) for k in range(1, ne)]
    cells = laid(mesh_state_choice, earlier_voltage, regions, dopant_charge_field, rows, beyond)
    while len(terms) > 1:
        terms = [terms[2 * k] + terms[2 * k + 1] for k in range(len(terms) // 2)]
    tables = terms[0]
    beside = []
    for odd_first in (False, True):
        at_low = odd_s if not odd_first else 1 - odd_s
        edge = jnp.where(at_low == 1, tables[0], tables[-1])
        beside.append(lax.ppermute(edge, "space", pairs("space", odd_first)))

    change, most = swept(tables, beside, cells, own)
    parts = {0: change}
    for k in range(2, ne, 2):
        parts[k] = toggled(change, "energy", k)
    parts[1] = toggled(change, "energy", 1)
    most = lax.all_to_all(most, ("energy", "space"), 0, 0)
    far = [parts[k] for k in range(2, ne, 2)]
    most, far = lax.optimization_barrier((most, far))
    for k, part in zip(range(2, ne, 2), far):
        parts[k ^ 1] = toggled(part, "energy", 1)
    return settled(most, earlier_voltage, [parts[k] for k in range(ne)])


def solution(mesh):
    placed = (
        P("energy", "space", None, None, None),
        P("energy", "space", None, None),
        P("space", None, None),
        P("space", "energy", None),
        P("space", "energy", None),
        P("space", None, None),
    )
    return jax.shard_map(
        on_device, mesh=mesh, in_specs=placed, out_specs=P("space", None, None), check_vma=False
    )
```

```python
import functools

import jax
import jax.numpy as jnp
from jax import lax
from jax.experimental import pallas as pl
from jax.experimental.pallas import tpu as pltpu
from jax.sharding import PartitionSpec as P

PL = 16
SWEEPS = 4
HALO = 4
PAD = 8
LANES = 128
SUB = 8
MIB = 1 << 20
BLOCK = 16
LOOK = 16
LAY = 16
SETTLE = 4
EDGE_COST = 10 * MIB
TABLE_COST = 10 * MIB
LAY_COST = 3 * MIB
LATER = pl.ANY
PAIRS = 16


def merge(parts, width):
    lane = lax.broadcasted_iota(jnp.int32, (SUB, LANES), 1)
    while len(parts) > 1:
        low = (lane & width) == 0
        merged = []
        for a, b in zip(parts[::2], parts[1::2]):
            merged.append(jnp.where(low, a, b) + pltpu.roll(jnp.where(low, b, a), width, 1))
        parts = merged
        width *= 2
    return parts[0]


def table_kernel(green_ref, inject_ref, rows1_ref, rows2_ref, out_ref, packed1_ref, packed2_ref, part_ref):
    slabs, _, states, columns = green_ref.shape
    chunks = columns // LANES
    groups = states // SUB
    for packed_ref, rows_ref in ((packed1_ref, rows1_ref), (packed2_ref, rows2_ref)):
        packed_ref[2 * slabs * SUB :] = rows_ref[...]
    for slab in range(slabs):
        weights = [
            [
                jnp.broadcast_to(inject_ref[slab, c : c + 1, k * LANES : (k + 1) * LANES], (SUB, LANES))
                for k in range(chunks)
            ]
            for c in range(2)
        ]

        def some_groups(i, _, slab=slab, weights=weights):
            for pair in range(PAIRS):
                sums = [[], []]
                for g in range(2):
                    rows = pl.ds(pl.multiple_of((i * (2 * PAIRS) + 2 * pair + g) * SUB, SUB), SUB)
                    total = [None, None]
                    for k in range(chunks):
                        cols = slice(k * LANES, (k + 1) * LANES)
                        re = green_ref[slab, 0, rows, cols]
                        im = green_ref[slab, 1, rows, cols]
                        squared = re * re + im * im
                        for c in range(2):
                            term = squared * weights[c][k]
                            total[c] = term if total[c] is None else total[c] + term
                    for c in range(2):
                        sums[c].append(total[c])
                for c in range(2):
                    part_ref[slab, c, i * PAIRS + pair] = merge(sums[c], 1)
            return _

        lax.fori_loop(0, groups // (2 * PAIRS), some_groups, None)
    lane = lax.broadcasted_iota(jnp.int32, (SUB, LANES), 1)
    count, width = groups // 2, 2
    while count > 1:
        low = (lane & width) == 0
        count //= 2
        for slab in range(slabs):
            for c in range(2):
                for k in range(count):
                    a, b = part_ref[slab, c, 2 * k], part_ref[slab, c, 2 * k + 1]
                    both = jnp.where(low, a, b) + pltpu.roll(jnp.where(low, b, a), width, 1)
                    if count > 1:
                        part_ref[slab, c, k] = both
                    else:
                        out_ref[slab, c] = both
                        at = (2 * slab + c) * SUB
                        packed1_ref[at : at + SUB] = both
                        packed2_ref[at : at + SUB] = both
        width *= 2


def orbital_table(green, inject, rows):
    slabs, _, states, _ = green.shape
    vmem = pl.BlockSpec(memory_space=pltpu.VMEM)
    packed = jax.ShapeDtypeStruct((2 * slabs * SUB + rows[0].shape[0], LANES), jnp.float32)
    return pl.pallas_call(
        table_kernel,
        in_specs=[vmem] * 4,
        out_specs=[vmem] * 3,
        out_shape=[jax.ShapeDtypeStruct((slabs, 2, SUB, LANES), jnp.float32), packed, packed],
        scratch_shapes=[pltpu.VMEM((slabs, 2, states // SUB // 2, SUB, LANES), jnp.float32)],
        compiler_params=pltpu.CompilerParams(vmem_limit_bytes=20 * MIB),
        cost_estimate=pl.CostEstimate(flops=0, bytes_accessed=TABLE_COST, transcendentals=0),
        name="table",
    )(green, inject, *rows)


def lookup(tables, choice):
    lane = choice >> 3
    group = choice & (SUB - 1)
    bits = [(group & (1 << b)) != 0 for b in range(3)]
    out = []
    for table in tables:
        found = [jnp.take_along_axis(t, lane, axis=1, mode="promise_in_bounds") for t in table]
        for bit in bits:
            found = [jnp.where(bit, found[2 * k + 1], found[2 * k]) for k in range(len(found) // 2)]
        out.append(found[0])
    return out


def permittivity(regions):
    return jnp.where(regions == 0, 1.0, jnp.where(regions == 1, 0.33, 1.7)).astype(jnp.float32)


def grouped(count, size, step, carry):
    odd = count % size
    if odd:
        carry = step(0, odd, carry)
    return lax.fori_loop(0, count // size, lambda i, c: step(odd + i * size, size, c), carry)


def around(center, below, above, left, right):
    lane = lax.broadcasted_iota(jnp.int32, (SUB, LANES), 1)
    after = jnp.where(lane < LANES - 1, pltpu.roll(center, LANES - 1, 1), 0.0)
    ahead = jnp.where(lane > 0, pltpu.roll(center, 1, 1), 0.0)
    return above + below + right + left + after + ahead


def position():
    return lax.axis_index("energy"), lax.axis_index("space"), lax.axis_size("energy"), lax.axis_size("space")


NEAR = HALO - 1


def edge_kernel(
    regions_ref, dopant_ref, mesh_ref, old_ref, green_ref, inject_ref,
    rows1_ref, rows2_ref, planes1_ref, planes2_ref,
    regions_s, dopant_s, mesh_s, old_s, sems,
):
    e, s, ne, _ = position()
    odd_e, odd_s = (e & 1) == 1, (s & 1) == 1
    planes, own, _ = regions_s.shape
    pieces = [(regions_ref, regions_s), (dopant_ref, dopant_s)]
    for source, held in ((mesh_ref, mesh_s), (old_ref, old_s)):
        pieces.append((source.at[0:HALO], held.at[0]))
        pieces.append((source.at[planes - HALO : planes], held.at[1]))
    copies = [pltpu.make_async_copy(a, b, sems.at[k]) for k, (a, b) in enumerate(pieces)]
    for copy in copies:
        copy.start()
    for copy in copies[:2]:
        copy.wait()
    top, bottom = slice(0, NEAR), slice(own - NEAR, own)
    for p in range(planes):
        for field, values in ((0, permittivity(regions_s[p])), (1, dopant_s[p])):
            at = (field * planes + p) * NEAR
            rows1_ref[at : at + NEAR] = jnp.where(odd_e, values[top], values[bottom])
            rows2_ref[at : at + NEAR] = jnp.where(odd_e, values[bottom], values[top])
    for copy in copies[2:]:
        copy.wait()
    row0 = pl.multiple_of(e * own, SUB)
    up_from = pl.multiple_of(jnp.maximum(row0 - SUB, 0), SUB)
    down_from = pl.multiple_of(jnp.minimum(row0 + own, mesh_s.shape[2] - SUB), SUB)
    span = own + 2 * HALO
    for out_ref, side in ((planes1_ref, jnp.where(odd_s, 0, 1)), (planes2_ref, jnp.where(odd_s, 1, 0))):
        for k in range(NEAR):
            p, at = k + side, k * span
            out_ref[at : at + HALO] = mesh_s[side, p, pl.ds(up_from, SUB)][SUB - HALO :].astype(jnp.float32)
            out_ref[at + HALO : at + HALO + own] = mesh_s[side, p, pl.ds(row0, own)].astype(jnp.float32)
            out_ref[at + HALO + own : at + span] = mesh_s[side, p, pl.ds(down_from, SUB)][:HALO].astype(jnp.float32)
            low = planes - NEAR + k
            for field, at in ((0, (NEAR + HALO) * span + k * own), (1, (NEAR + HALO) * span + (NEAR + k) * own)):
                held = regions_s if field == 0 else dopant_s
                values = jnp.where(side == 0, held[k], held[low])
                out_ref[at : at + own] = permittivity(values) if field == 0 else values
        for k in range(HALO):
            at = (NEAR + k) * span
            out_ref[at : at + HALO] = jnp.where(e > 0, old_s[side, k, pl.ds(up_from, SUB)][SUB - HALO :], 0.0)
            out_ref[at + HALO : at + HALO + own] = old_s[side, k, pl.ds(row0, own)]
            out_ref[at + HALO + own : at + span] = jnp.where(
                e < ne - 1, old_s[side, k, pl.ds(down_from, SUB)][:HALO], 0.0
            )


def edges(regions, dopant, mesh, old, green, inject):
    planes, own, lanes = regions.shape
    rows = jax.ShapeDtypeStruct((2 * NEAR * planes, lanes), jnp.float32)
    cells = jax.ShapeDtypeStruct(((NEAR + HALO) * (own + 2 * HALO) + 2 * NEAR * own, lanes), jnp.float32)
    held = (2, HALO) + mesh.shape[1:]
    outs = pl.pallas_call(
        edge_kernel,
        in_specs=[pl.BlockSpec(memory_space=pl.ANY)] * 6,
        out_specs=[pl.BlockSpec(memory_space=pltpu.VMEM)] * 4,
        out_shape=[rows, rows, cells, cells],
        scratch_shapes=[
            pltpu.VMEM(regions.shape, jnp.int32),
            pltpu.VMEM(regions.shape, jnp.float32),
            pltpu.VMEM(held, jnp.int32),
            pltpu.VMEM(held, jnp.float32),
            pltpu.SemaphoreType.DMA((6,)),
        ],
        compiler_params=pltpu.CompilerParams(vmem_limit_bytes=8 * MIB),
        cost_estimate=pl.CostEstimate(flops=0, bytes_accessed=EDGE_COST, transcendentals=0),
        name="edges",
    )(*(pltpu.with_memory_space_constraint(x, pltpu.HBM) for x in (regions, dopant, mesh, old, green, inject)))
    return outs[:2], outs[2:]


def beside_rows(rows1_ref, rows2_ref, at):
    e, _, ne, _ = position()
    odd = (e & 1) == 1
    one = rows1_ref[at : at + NEAR]
    two = jnp.where((e > 0) & (e < ne - 1), rows2_ref[at : at + NEAR], 0.0)
    return jnp.where(odd, one, two), jnp.where(odd, two, one)


def join_kernel(*refs):
    rows1_ref, rows2_ref = refs[-5:-3]
    tables_ref, first_ref, second_ref = refs[-3:]
    odd_s = (lax.axis_index("space") & 1) == 1
    slabs = tables_ref.shape[0]
    ahead = 2 * slabs * SUB
    planes = (rows1_ref.shape[0] - ahead) // (2 * NEAR)
    tables = []
    for slab in range(slabs):
        for c in range(2):
            at = (2 * slab + c) * SUB
            terms = [ref[slab, c] if len(ref.shape) == 4 else ref[at : at + SUB] for ref in refs[:-5]]
            while len(terms) > 1:
                terms = [a + b for a, b in zip(terms[::2], terms[1::2])]
            tables_ref[slab, c] = terms[0]
            tables.append(terms[0])
    for k in range(NEAR):
        for field in range(2):
            low = beside_rows(rows1_ref, rows2_ref, ahead + (field * planes + k) * NEAR)
            high = beside_rows(rows1_ref, rows2_ref, ahead + (field * planes + planes - NEAR + k) * NEAR)
            top = (field * NEAR + k) * SUB
            for at, a, b in zip((top + 1, top + HALO), low, high):
                first_ref[at : at + NEAR] = jnp.where(odd_s, a, b)
                second_ref[at : at + NEAR] = jnp.where(odd_s, b, a)
    for c in range(2):
        top = (2 * NEAR + c) * SUB
        low, high = tables[c], tables[2 * (slabs - 1) + c]
        first_ref[top : top + SUB] = jnp.where(odd_s, low, high)
        second_ref[top : top + SUB] = jnp.where(odd_s, high, low)


def joined(terms, rows):
    vmem = pl.BlockSpec(memory_space=pltpu.VMEM)
    packed = jax.ShapeDtypeStruct((2 * (NEAR + 1) * SUB, LANES), jnp.float32)
    outs = pl.pallas_call(
        join_kernel,
        in_specs=[vmem] * (len(terms) + 2),
        out_specs=[vmem] * 3,
        out_shape=[jax.ShapeDtypeStruct(terms[0].shape, jnp.float32), packed, packed],
        compiler_params=pltpu.CompilerParams(vmem_limit_bytes=8 * MIB),
        name="join",
    )(*terms, *rows)
    return outs[0], outs[1:]


def broadcast_table(slab_value):
    return [[jnp.broadcast_to(slab_value[c, g : g + 1], (SUB, LANES)) for g in range(SUB)] for c in range(2)]


def first_sweep(choice, tables, center, bend, permit, dopant, outside):
    electrons, holes = lookup(tables, choice)
    if outside is not None:
        electrons, holes = jnp.where(outside, 1.0, electrons), jnp.where(outside, 1.0, holes)
    mismatch = permit * bend - (dopant + holes - electrons)
    jacobian = 6.0 * permit + electrons + holes
    return electrons, holes, center - mismatch / jacobian


def outside_rows(r, span):
    e, _, ne, _ = position()
    row = lax.broadcasted_iota(jnp.int32, (SUB, LANES), 0)
    outside = None
    if r == 0:
        outside = (row < HALO) & (e == 0)
    if r == span - SUB:
        below = (row >= SUB - HALO) & (e == ne - 1)
        outside = below if outside is None else outside | below
    return outside


def lay_kernel(mesh_ref, old_ref, planes1_ref, planes2_ref, mesh_x, before_x, bend_x):
    e, s, ne, _ = position()
    odd_s = (s & 1) == 1
    planes, span, _ = mesh_x.shape
    own = span - 2 * HALO
    row0 = pl.multiple_of(e * own, SUB)
    up, mid, down = slice(0, HALO), slice(HALO, HALO + own), slice(HALO + own, span)
    up_b, mid_b, down_b = (slice(PAD + x.start, PAD + x.stop) for x in (up, mid, down))
    up_from = pl.multiple_of(jnp.maximum(row0 - SUB, 0), SUB)
    down_from = pl.multiple_of(jnp.minimum(row0 + own, mesh_ref.shape[1] - SUB), SUB)

    def lay(first, count, _):
        for k in range(count):
            p = first + k
            q = p + HALO
            mesh_x[p, mid] = mesh_ref[p, pl.ds(row0, own)]
            mesh_x[p, up] = mesh_ref[p, pl.ds(up_from, SUB)][SUB - HALO :]
            mesh_x[p, down] = mesh_ref[p, pl.ds(down_from, SUB)][:HALO]
            before_x[q, mid_b] = old_ref[p, pl.ds(row0, own)]
            before_x[q, up_b] = jnp.where(e > 0, old_ref[p, pl.ds(up_from, SUB)][SUB - HALO :], 0.0)
            before_x[q, down_b] = jnp.where(e < ne - 1, old_ref[p, pl.ds(down_from, SUB)][:HALO], 0.0)
        return _

    grouped(planes, LAY, lay, None)
    for k in range(HALO):
        at = (NEAR + k) * span
        a, b = planes1_ref[at : at + span], planes2_ref[at : at + span]
        before_x[k, PAD : PAD + span] = jnp.where(odd_s, a, b)
        before_x[HALO + planes + k, PAD : PAD + span] = jnp.where(odd_s, b, a)

    def bends(first, count, _):
        for r in range(0, span, SUB):
            at = PAD + r
            held = [before_x[HALO + first + k, at : at + SUB] for k in range(-1, count + 1)]
            for k in range(count):
                q = HALO + first + k
                neighbours = around(
                    held[k + 1], held[k], held[k + 2],
                    before_x[q, at - 1 : at - 1 + SUB], before_x[q, at + 1 : at + 1 + SUB],
                )
                bend_x[first + k, r : r + SUB] = 6.0 * held[k + 1] - neighbours
        return _

    grouped(planes, BLOCK, bends, None)


def laid(mesh, old, beyond, own):
    planes, _, lanes = mesh.shape
    cells = (planes, own + 2 * HALO, lanes)
    padded = (planes + 2 * HALO, own + 2 * HALO + 2 * PAD, lanes)
    vmem = pl.BlockSpec(memory_space=pltpu.VMEM)
    f32 = jnp.float32
    return pl.pallas_call(
        lay_kernel,
        in_specs=[vmem] * 4,
        out_specs=[vmem] * 3,
        out_shape=[jax.ShapeDtypeStruct(*x) for x in ((cells, jnp.int32), (padded, f32), (cells, f32))],
        compiler_params=pltpu.CompilerParams(vmem_limit_bytes=16 * MIB),
        cost_estimate=pl.CostEstimate(flops=0, bytes_accessed=LAY_COST, transcendentals=0),
        name="lay",
    )(mesh, old, *beyond)


def own_kernel(
    tables_ref, mesh_x, before_x, bend_x, regions_ref, dopant_ref, rows1_ref, rows2_ref,
    permit_x, dopant_x, electron_x, hole_x, now_x,
):
    planes, own, _ = regions_ref.shape
    slabs = tables_ref.shape[0]
    span = own + 2 * HALO
    up, mid, down = slice(HALO - NEAR, HALO), slice(HALO, HALO + own), slice(HALO + own, HALO + own + NEAR)
    for p in range(planes):
        permit_x[p, mid] = permittivity(regions_ref[p])
        dopant_x[p, mid] = dopant_ref[p]
        for field, field_x in ((0, permit_x), (1, dopant_x)):
            at = 2 * slabs * SUB + (field * planes + p) * NEAR
            field_x[p, up], field_x[p, down] = beside_rows(rows1_ref, rows2_ref, at)
    for slab in range(slabs):
        tables = broadcast_table(tables_ref[slab])

        def some(first, count, _, tables=tables, slab=slab):
            for r in range(0, span, SUB):
                at, rows = PAD + r, slice(r, r + SUB)
                for k in range(count):
                    p = slab * PL + first + k
                    electron_x[p, rows], hole_x[p, rows], now_x[p, rows] = first_sweep(
                        mesh_x[p, rows], tables, before_x[HALO + p, at : at + SUB], bend_x[p, rows],
                        permit_x[p, rows], dopant_x[p, rows], outside_rows(r, span),
                    )
            return _

        grouped(PL, LOOK, some, None)


def own_planes(tables, laid_out, regions, dopant, rows):
    vmem = pl.BlockSpec(memory_space=pltpu.VMEM)
    cells = laid_out[0].shape
    return pl.pallas_call(
        own_kernel,
        in_specs=[vmem] * 8,
        out_specs=[vmem] * 5,
        out_shape=[jax.ShapeDtypeStruct(cells, jnp.float32)] * 5,
        compiler_params=pltpu.CompilerParams(vmem_limit_bytes=16 * MIB),
        cost_estimate=pl.CostEstimate(flops=0, bytes_accessed=LAY_COST, transcendentals=0),
        name="own",
    )(tables, *laid_out, regions, dopant, *rows)


def sweep_kernel(
    packed1_ref, packed2_ref, planes1_ref, planes2_ref, before_x, permit_o, dopant_o, electron_o, hole_o, now_o,
    change_ref, most_ref, permit_x, dopant_x, electron_x, hole_x, now_s, next_s,
):
    _, s, _, ns = position()
    odd_s = (s & 1) == 1
    planes, own, _ = change_ref.shape
    span = own + 2 * HALO
    tops = range(0, span, SUB)

    def bring(first, count, _):
        for k in range(count):
            p = first + k
            q = HALO + p
            for r in tops:
                rows = slice(r, r + SUB)
                permit_x[q, rows] = permit_o[p, rows]
                dopant_x[q, rows] = dopant_o[p, rows]
                electron_x[q, rows] = electron_o[p, rows]
                hole_x[q, rows] = hole_o[p, rows]
                now_s[q, PAD + r : PAD + r + SUB] = now_o[p, rows]
        return _

    grouped(planes, LAY, bring, None)
    for low in (True, False):
        a, b = (packed1_ref, packed2_ref) if low else (packed2_ref, packed1_ref)
        c, d = (planes1_ref, planes2_ref) if low else (planes2_ref, planes1_ref)
        inside = s > 0 if low else s < ns - 1
        top = 2 * NEAR * SUB
        tables = [
            [
                jnp.where(
                    inside,
                    jnp.where(
                        odd_s,
                        jnp.broadcast_to(a[t + g : t + g + 1], (SUB, LANES)),
                        jnp.broadcast_to(b[t + g : t + g + 1], (SUB, LANES)),
                    ),
                    1.0,
                )
                for g in range(SUB)
            ]
            for t in (top, top + SUB)
        ]
        for k in range(NEAR):
            q = 1 + k if low else HALO + planes + k
            for field, field_x in ((0, permit_x), (1, dopant_x)):
                t = (field * NEAR + k) * SUB
                m = (NEAR + HALO) * span + (field * NEAR + k) * own
                field_x[q, :HALO] = jnp.where(odd_s, a[t : t + HALO], b[t : t + HALO])
                field_x[q, HALO : HALO + own] = jnp.where(odd_s, c[m : m + own], d[m : m + own])
                field_x[q, HALO + own :] = jnp.where(odd_s, a[t + HALO : t + SUB], b[t + HALO : t + SUB])
            for r in tops:
                at, rows = PAD + r, slice(r, r + SUB)
                here = slice(k * span + r, k * span + r + SUB)
                permit, dopant = permit_x[q, rows], dopant_x[q, rows]
                choice = jnp.where(odd_s, c[here], d[here]).astype(jnp.int32)
                center = before_x[q, at : at + SUB]
                neighbours = around(
                    center, before_x[q - 1, at : at + SUB], before_x[q + 1, at : at + SUB],
                    before_x[q, at - 1 : at - 1 + SUB], before_x[q, at + 1 : at + 1 + SUB],
                )
                electrons, holes, fresh = first_sweep(
                    choice, tables, center, 6.0 * center - neighbours, permit, dopant, outside_rows(r, span)
                )
                electron_x[q, rows] = electrons
                hole_x[q, rows] = holes
                now_s[q, at : at + SUB] = fresh

    source = now_s
    for sweep in range(1, SWEEPS):
        final = sweep == SWEEPS - 1
        target = next_s if source is now_s else now_s
        starts = range(HALO, HALO + own, SUB) if final else tops

        def step(first, count, most, sweep=sweep, source=source, target=target, starts=starts, final=final):
            for r in starts:
                rows = slice(r, r + SUB)
                at = PAD + r
                rows_b = slice(at, at + SUB)
                held = [source[1 + sweep + first + k, rows_b] for k in range(-1, count + 1)]
                for k in range(count):
                    q = 1 + sweep + first + k
                    center = held[k + 1]
                    neighbours = around(
                        center, held[k], held[k + 2],
                        source[q, at - 1 : at - 1 + SUB], source[q, at + 1 : at + 1 + SUB],
                    )
                    permit = permit_x[q, rows]
                    before = before_x[q, rows_b]
                    moved = center - before
                    electrons = electron_x[q, rows] * jnp.exp(moved)
                    holes = hole_x[q, rows] * jnp.exp(-moved)
                    mismatch = permit * (6.0 * center - neighbours) - (dopant_x[q, rows] + holes - electrons)
                    jacobian = 6.0 * permit + electrons + holes
                    fresh = center - mismatch / jacobian
                    if final:
                        change = fresh - before
                        change_ref[q - HALO, r - HALO : r - HALO + SUB] = change
                        most = jnp.maximum(most, jnp.abs(change))
                    else:
                        target[q, rows_b] = fresh
            return most

        most = grouped(planes + 2 * (SWEEPS - 1 - sweep), BLOCK, step, jnp.zeros((SUB, LANES), jnp.float32))
        if final:
            most_ref[...] = jnp.broadcast_to(jnp.max(most, axis=0, keepdims=True)[None], most_ref.shape)
        source = target


def swept(packed, beyond, fields, own):
    planes, span, lanes = fields[1].shape
    padded = fields[0].shape
    cells = (padded[0], span, lanes)
    vmem = pl.BlockSpec(memory_space=pltpu.VMEM)
    f32 = jnp.float32
    return pl.pallas_call(
        sweep_kernel,
        in_specs=[vmem] * 10,
        out_specs=[vmem, vmem],
        out_shape=[
            jax.ShapeDtypeStruct((planes, own, lanes), f32),
            jax.ShapeDtypeStruct((lax.axis_size(("energy", "space")), 1, lanes), f32),
        ],
        scratch_shapes=[pltpu.VMEM(cells, f32)] * 4 + [pltpu.VMEM(padded, f32)] * 2,
        compiler_params=pltpu.CompilerParams(vmem_limit_bytes=24 * MIB),
        name="sweeps",
    )(*packed, *beyond, *fields)


def settle_kernel(most_ref, old_ref, *rest):
    parts, out_ref, result, sems = rest[:-3], rest[-3], rest[-2], rest[-1]
    e = lax.axis_index("energy")
    planes, own, _ = parts[0].shape
    scale = 1.0 / (1.0 + jnp.max(most_ref[...]))
    size = planes // SETTLE
    copies = []
    for b in range(SETTLE):
        at = slice(b * size, (b + 1) * size)
        for k, part in enumerate(parts):
            rows = pl.ds(pl.multiple_of((e ^ k) * own, SUB), own)
            result[at, rows] = old_ref[at, rows] + part[at] * scale
        copies.append(pltpu.make_async_copy(result.at[at], out_ref.at[at], sems.at[b]))
        copies[-1].start()
    for copy in copies:
        copy.wait()


def settled(most, old, parts):
    vmem = pl.BlockSpec(memory_space=pltpu.VMEM)
    return pl.pallas_call(
        settle_kernel,
        in_specs=[vmem] * (2 + len(parts)),
        out_specs=pl.BlockSpec(memory_space=pl.ANY),
        out_shape=jax.ShapeDtypeStruct(old.shape, jnp.float32),
        scratch_shapes=[pltpu.VMEM(old.shape, jnp.float32), pltpu.SemaphoreType.DMA((SETTLE,))],
        compiler_params=pltpu.CompilerParams(vmem_limit_bytes=16 * MIB),
        name="settle",
    )(most, old, *parts)


def pairs(axis, odd_first):
    count = lax.axis_size(axis)
    out = []
    for low in range(1 if odd_first else 0, count - 1, 2):
        out += [(low, low + 1), (low + 1, low)]
    return out


def toggled(x, axis, mask):
    return lax.ppermute(x, axis, [(i, i ^ mask) for i in range(lax.axis_size(axis))])


def on_device(green_blocks, injection, mesh_state_choice, regions, dopant_charge_field, earlier_voltage):
    ne = lax.axis_size("energy")
    own = regions.shape[1]
    green, inject = green_blocks[0], injection[0]

    def exchanged(sent, axis):
        return [lax.ppermute(x, axis, pairs(axis, odd_first)) for x, odd_first in zip(sent, (False, True))]

    rows, beyond = edges(regions, dopant_charge_field, mesh_state_choice, earlier_voltage, green, inject)
    beyond = exchanged(beyond, "space")
    tables, packed1, packed2 = orbital_table(green, inject, rows)
    (tables, packed1, packed2), beyond = lax.optimization_barrier(((tables, packed1, packed2), beyond))
    second = [k for k in range(3, ne) if k & (k + 1) == 0]
    terms = [tables]
    for k in range(1, ne):
        sent = packed1 if k == 1 else packed2 if k in second else tables
        terms.append(toggled(sent, "energy", k))
    e = lax.axis_index("energy")
    partner = jnp.where(e & 1 == 1, e + 1, e - 1)
    rows = [terms[1], terms[3]]
    for k in second[1:]:
        rows[1] = jnp.where(e ^ partner == k, terms[k], rows[1])
    laid_out = laid(mesh_state_choice, earlier_voltage, beyond, own)
    terms, laid_out = lax.optimization_barrier((terms, laid_out))
    tables, packed = joined(terms, rows)
    packed = exchanged(packed, "space")
    fields = own_planes(tables, laid_out, regions, dopant_charge_field, rows)
    change, most = swept(packed, beyond, (laid_out[1], *fields), own)
    parts = {0: change}
    for k in range(2, ne, 2):
        parts[k] = toggled(change, "energy", k)
    parts[1] = toggled(change, "energy", 1)
    most = lax.all_to_all(most, ("energy", "space"), 0, 0)
    far = [parts[k] for k in range(2, ne, 2)]
    most, far = lax.optimization_barrier((most, far))
    for k, part in zip(range(2, ne, 2), far):
        parts[k ^ 1] = toggled(part, "energy", 1)
    return settled(most, earlier_voltage, [parts[k] for k in range(ne)])


def solution(mesh):
    placed = (
        P("energy", "space", None, None, None),
        P("energy", "space", None, None),
        P("space", None, None),
        P("space", "energy", None),
        P("space", "energy", None),
        P("space", None, None),
    )
    return jax.shard_map(
        on_device, mesh=mesh, in_specs=placed, out_specs=P("space", None, None), check_vma=False
    )
```

```python
import functools

import jax
import jax.numpy as jnp
from jax import lax
from jax.experimental import pallas as pl
from jax.experimental.pallas import tpu as pltpu
from jax.sharding import PartitionSpec as P

PL = 16
SWEEPS = 4
HALO = 4
PAD = 8
LANES = 128
SUB = 8
MIB = 1 << 20
BLOCK = 32
LOOK = 16
LAY = 16
SETTLE = 2
EDGE_COST = 10 * MIB
TABLE_COST = 10 * MIB
LAY_COST = 3 * MIB
LATER = pl.ANY
PAIRS = 64


def merge(parts, width):
    lane = lax.broadcasted_iota(jnp.int32, (SUB, LANES), 1)
    while len(parts) > 1:
        low = (lane & width) == 0
        merged = []
        for a, b in zip(parts[::2], parts[1::2]):
            merged.append(jnp.where(low, a, b) + pltpu.roll(jnp.where(low, b, a), width, 1))
        parts = merged
        width *= 2
    return parts[0]


def table_kernel(green_ref, inject_ref, rows1_ref, rows2_ref, out_ref, packed1_ref, packed2_ref, part_ref):
    slabs, _, states, columns = green_ref.shape
    chunks = columns // LANES
    groups = states // SUB
    for packed_ref, rows_ref in ((packed1_ref, rows1_ref), (packed2_ref, rows2_ref)):
        packed_ref[2 * slabs * SUB :] = rows_ref[...]
    for slab in range(slabs):
        weights = [
            [
                jnp.broadcast_to(inject_ref[slab, c : c + 1, k * LANES : (k + 1) * LANES], (SUB, LANES))
                for k in range(chunks)
            ]
            for c in range(2)
        ]

        def some_groups(i, _, slab=slab, weights=weights):
            for pair in range(PAIRS):
                sums = [[], []]
                for g in range(2):
                    rows = pl.ds(pl.multiple_of((i * (2 * PAIRS) + 2 * pair + g) * SUB, SUB), SUB)
                    total = [None, None]
                    for k in range(chunks):
                        cols = slice(k * LANES, (k + 1) * LANES)
                        re = green_ref[slab, 0, rows, cols]
                        im = green_ref[slab, 1, rows, cols]
                        squared = re * re + im * im
                        for c in range(2):
                            term = squared * weights[c][k]
                            total[c] = term if total[c] is None else total[c] + term
                    for c in range(2):
                        sums[c].append(total[c])
                for c in range(2):
                    part_ref[slab, c, i * PAIRS + pair] = merge(sums[c], 1)
            return _

        lax.fori_loop(0, groups // (2 * PAIRS), some_groups, None)
    lane = lax.broadcasted_iota(jnp.int32, (SUB, LANES), 1)
    count, width = groups // 2, 2
    while count > 1:
        low = (lane & width) == 0
        count //= 2
        for slab in range(slabs):
            for c in range(2):
                for k in range(count):
                    a, b = part_ref[slab, c, 2 * k], part_ref[slab, c, 2 * k + 1]
                    both = jnp.where(low, a, b) + pltpu.roll(jnp.where(low, b, a), width, 1)
                    if count > 1:
                        part_ref[slab, c, k] = both
                    else:
                        out_ref[slab, c] = both
                        at = (2 * slab + c) * SUB
                        packed1_ref[at : at + SUB] = both
                        packed2_ref[at : at + SUB] = both
        width *= 2


def orbital_table(green, inject, rows):
    slabs, _, states, _ = green.shape
    vmem = pl.BlockSpec(memory_space=pltpu.VMEM)
    packed = jax.ShapeDtypeStruct((2 * slabs * SUB + rows[0].shape[0], LANES), jnp.float32)
    return pl.pallas_call(
        table_kernel,
        in_specs=[vmem] * 4,
        out_specs=[vmem] * 3,
        out_shape=[jax.ShapeDtypeStruct((slabs, 2, SUB, LANES), jnp.float32), packed, packed],
        scratch_shapes=[pltpu.VMEM((slabs, 2, states // SUB // 2, SUB, LANES), jnp.float32)],
        compiler_params=pltpu.CompilerParams(vmem_limit_bytes=20 * MIB),
        cost_estimate=pl.CostEstimate(flops=0, bytes_accessed=TABLE_COST, transcendentals=0),
        name="table",
    )(green, inject, *rows)


def lookup(tables, choice):
    lane = choice >> 3
    group = choice & (SUB - 1)
    bits = [(group & (1 << b)) != 0 for b in range(3)]
    out = []
    for table in tables:
        found = [jnp.take_along_axis(t, lane, axis=1, mode="promise_in_bounds") for t in table]
        for bit in bits:
            found = [jnp.where(bit, found[2 * k + 1], found[2 * k]) for k in range(len(found) // 2)]
        out.append(found[0])
    return out


def permittivity(regions):
    return jnp.where(regions == 0, 1.0, jnp.where(regions == 1, 0.33, 1.7)).astype(jnp.float32)


def grouped(count, size, step, carry):
    odd = count % size
    if odd:
        carry = step(0, odd, carry)
    return lax.fori_loop(0, count // size, lambda i, c: step(odd + i * size, size, c), carry)


def around(center, below, above, left, right):
    lane = lax.broadcasted_iota(jnp.int32, (SUB, LANES), 1)
    after = jnp.where(lane < LANES - 1, pltpu.roll(center, LANES - 1, 1), 0.0)
    ahead = jnp.where(lane > 0, pltpu.roll(center, 1, 1), 0.0)
    return above + below + right + left + after + ahead


def position():
    return lax.axis_index("energy"), lax.axis_index("space"), lax.axis_size("energy"), lax.axis_size("space")


NEAR = HALO - 1


def edge_kernel(
    regions_ref, dopant_ref, mesh_ref, old_ref, green_ref, inject_ref,
    rows1_ref, rows2_ref, planes1_ref, planes2_ref,
    regions_s, dopant_s, mesh_s, old_s, sems,
):
    e, s, ne, _ = position()
    odd_e, odd_s = (e & 1) == 1, (s & 1) == 1
    planes, own, _ = regions_s.shape
    pieces = [(regions_ref, regions_s), (dopant_ref, dopant_s)]
    for source, held in ((mesh_ref, mesh_s), (old_ref, old_s)):
        pieces.append((source.at[0:HALO], held.at[0]))
        pieces.append((source.at[planes - HALO : planes], held.at[1]))
    copies = [pltpu.make_async_copy(a, b, sems.at[k]) for k, (a, b) in enumerate(pieces)]
    for copy in copies:
        copy.start()
    for copy in copies[:2]:
        copy.wait()
    top, bottom = slice(0, NEAR), slice(own - NEAR, own)
    for p in range(planes):
        for field, values in ((0, permittivity(regions_s[p])), (1, dopant_s[p])):
            at = (field * planes + p) * NEAR
            rows1_ref[at : at + NEAR] = jnp.where(odd_e, values[top], values[bottom])
            rows2_ref[at : at + NEAR] = jnp.where(odd_e, values[bottom], values[top])
    for copy in copies[2:]:
        copy.wait()
    row0 = pl.multiple_of(e * own, SUB)
    up_from = pl.multiple_of(jnp.maximum(row0 - SUB, 0), SUB)
    down_from = pl.multiple_of(jnp.minimum(row0 + own, mesh_s.shape[2] - SUB), SUB)
    span = own + 2 * HALO
    for out_ref, side in ((planes1_ref, jnp.where(odd_s, 0, 1)), (planes2_ref, jnp.where(odd_s, 1, 0))):
        for k in range(NEAR):
            p, at = k + side, k * span
            out_ref[at : at + HALO] = mesh_s[side, p, pl.ds(up_from, SUB)][SUB - HALO :].astype(jnp.float32)
            out_ref[at + HALO : at + HALO + own] = mesh_s[side, p, pl.ds(row0, own)].astype(jnp.float32)
            out_ref[at + HALO + own : at + span] = mesh_s[side, p, pl.ds(down_from, SUB)][:HALO].astype(jnp.float32)
            low = planes - NEAR + k
            for field, at in ((0, (NEAR + HALO) * span + k * own), (1, (NEAR + HALO) * span + (NEAR + k) * own)):
                held = regions_s if field == 0 else dopant_s
                values = jnp.where(side == 0, held[k], held[low])
                out_ref[at : at + own] = permittivity(values) if field == 0 else values
        for k in range(HALO):
            at = (NEAR + k) * span
            out_ref[at : at + HALO] = jnp.where(e > 0, old_s[side, k, pl.ds(up_from, SUB)][SUB - HALO :], 0.0)
            out_ref[at + HALO : at + HALO + own] = old_s[side, k, pl.ds(row0, own)]
            out_ref[at + HALO + own : at + span] = jnp.where(
                e < ne - 1, old_s[side, k, pl.ds(down_from, SUB)][:HALO], 0.0
            )


def edges(regions, dopant, mesh, old, green, inject):
    planes, own, lanes = regions.shape
    rows = jax.ShapeDtypeStruct((2 * NEAR * planes, lanes), jnp.float32)
    cells = jax.ShapeDtypeStruct(((NEAR + HALO) * (own + 2 * HALO) + 2 * NEAR * own, lanes), jnp.float32)
    held = (2, HALO) + mesh.shape[1:]
    outs = pl.pallas_call(
        edge_kernel,
        in_specs=[pl.BlockSpec(memory_space=pl.ANY)] * 6,
        out_specs=[pl.BlockSpec(memory_space=pltpu.VMEM)] * 4,
        out_shape=[rows, rows, cells, cells],
        scratch_shapes=[
            pltpu.VMEM(regions.shape, jnp.int32),
            pltpu.VMEM(regions.shape, jnp.float32),
            pltpu.VMEM(held, jnp.int32),
            pltpu.VMEM(held, jnp.float32),
            pltpu.SemaphoreType.DMA((6,)),
        ],
        compiler_params=pltpu.CompilerParams(vmem_limit_bytes=8 * MIB),
        cost_estimate=pl.CostEstimate(flops=0, bytes_accessed=EDGE_COST, transcendentals=0),
        name="edges",
    )(*(pltpu.with_memory_space_constraint(x, pltpu.HBM) for x in (regions, dopant, mesh, old, green, inject)))
    return outs[:2], outs[2:]


def beside_rows(rows1_ref, rows2_ref, at):
    e, _, ne, _ = position()
    odd = (e & 1) == 1
    one = rows1_ref[at : at + NEAR]
    two = jnp.where((e > 0) & (e < ne - 1), rows2_ref[at : at + NEAR], 0.0)
    return jnp.where(odd, one, two), jnp.where(odd, two, one)


def join_kernel(*refs):
    rows1_ref, rows2_ref = refs[-5:-3]
    tables_ref, first_ref, second_ref = refs[-3:]
    odd_s = (lax.axis_index("space") & 1) == 1
    slabs = tables_ref.shape[0]
    ahead = 2 * slabs * SUB
    planes = (rows1_ref.shape[0] - ahead) // (2 * NEAR)
    tables = []
    for slab in range(slabs):
        for c in range(2):
            at = (2 * slab + c) * SUB
            terms = [ref[slab, c] if len(ref.shape) == 4 else ref[at : at + SUB] for ref in refs[:-5]]
            while len(terms) > 1:
                terms = [a + b for a, b in zip(terms[::2], terms[1::2])]
            tables_ref[slab, c] = terms[0]
            tables.append(terms[0])
    for k in range(NEAR):
        for field in range(2):
            low = beside_rows(rows1_ref, rows2_ref, ahead + (field * planes + k) * NEAR)
            high = beside_rows(rows1_ref, rows2_ref, ahead + (field * planes + planes - NEAR + k) * NEAR)
            top = (field * NEAR + k) * SUB
            for at, a, b in zip((top + 1, top + HALO), low, high):
                first_ref[at : at + NEAR] = jnp.where(odd_s, a, b)
                second_ref[at : at + NEAR] = jnp.where(odd_s, b, a)
    for c in range(2):
        top = (2 * NEAR + c) * SUB
        low, high = tables[c], tables[2 * (slabs - 1) + c]
        first_ref[top : top + SUB] = jnp.where(odd_s, low, high)
        second_ref[top : top + SUB] = jnp.where(odd_s, high, low)


def joined(terms, rows):
    vmem = pl.BlockSpec(memory_space=pltpu.VMEM)
    packed = jax.ShapeDtypeStruct((2 * (NEAR + 1) * SUB, LANES), jnp.float32)
    outs = pl.pallas_call(
        join_kernel,
        in_specs=[vmem] * (len(terms) + 2),
        out_specs=[vmem] * 3,
        out_shape=[jax.ShapeDtypeStruct(terms[0].shape, jnp.float32), packed, packed],
        compiler_params=pltpu.CompilerParams(vmem_limit_bytes=8 * MIB),
        name="join",
    )(*terms, *rows)
    return outs[0], outs[1:]


def broadcast_table(slab_value):
    return [[jnp.broadcast_to(slab_value[c, g : g + 1], (SUB, LANES)) for g in range(SUB)] for c in range(2)]


def first_sweep(choice, tables, center, bend, permit, dopant, outside):
    electrons, holes = lookup(tables, choice)
    if outside is not None:
        electrons, holes = jnp.where(outside, 1.0, electrons), jnp.where(outside, 1.0, holes)
    mismatch = permit * bend - (dopant + holes - electrons)
    jacobian = 6.0 * permit + electrons + holes
    return electrons, holes, center - mismatch / jacobian


def outside_rows(r, span):
    e, _, ne, _ = position()
    row = lax.broadcasted_iota(jnp.int32, (SUB, LANES), 0)
    outside = None
    if r == 0:
        outside = (row < HALO) & (e == 0)
    if r == span - SUB:
        below = (row >= SUB - HALO) & (e == ne - 1)
        outside = below if outside is None else outside | below
    return outside


def lay_kernel(mesh_ref, old_ref, planes1_ref, planes2_ref, mesh_x, before_x, bend_x):
    e, s, ne, _ = position()
    odd_s = (s & 1) == 1
    planes, span, _ = mesh_x.shape
    own = span - 2 * HALO
    row0 = pl.multiple_of(e * own, SUB)
    up, mid, down = slice(0, HALO), slice(HALO, HALO + own), slice(HALO + own, span)
    up_b, mid_b, down_b = (slice(PAD + x.start, PAD + x.stop) for x in (up, mid, down))
    up_from = pl.multiple_of(jnp.maximum(row0 - SUB, 0), SUB)
    down_from = pl.multiple_of(jnp.minimum(row0 + own, mesh_ref.shape[1] - SUB), SUB)

    def lay(first, count, _):
        for k in range(count):
            p = first + k
            q = p + HALO
            mesh_x[p, mid] = mesh_ref[p, pl.ds(row0, own)]
            mesh_x[p, up] = mesh_ref[p, pl.ds(up_from, SUB)][SUB - HALO :]
            mesh_x[p, down] = mesh_ref[p, pl.ds(down_from, SUB)][:HALO]
            before_x[q, mid_b] = old_ref[p, pl.ds(row0, own)]
            before_x[q, up_b] = jnp.where(e > 0, old_ref[p, pl.ds(up_from, SUB)][SUB - HALO :], 0.0)
            before_x[q, down_b] = jnp.where(e < ne - 1, old_ref[p, pl.ds(down_from, SUB)][:HALO], 0.0)
        return _

    grouped(planes, LAY, lay, None)
    for k in range(HALO):
        at = (NEAR + k) * span
        a, b = planes1_ref[at : at + span], planes2_ref[at : at + span]
        before_x[k, PAD : PAD + span] = jnp.where(odd_s, a, b)
        before_x[HALO + planes + k, PAD : PAD + span] = jnp.where(odd_s, b, a)

    def bends(first, count, _):
        for r in range(0, span, SUB):
            at = PAD + r
            held = [before_x[HALO + first + k, at : at + SUB] for k in range(-1, count + 1)]
            for k in range(count):
                q = HALO + first + k
                neighbours = around(
                    held[k + 1], held[k], held[k + 2],
                    before_x[q, at - 1 : at - 1 + SUB], before_x[q, at + 1 : at + 1 + SUB],
                )
                bend_x[first + k, r : r + SUB] = 6.0 * held[k + 1] - neighbours
        return _

    grouped(planes, BLOCK, bends, None)


def laid(mesh, old, beyond, own):
    planes, _, lanes = mesh.shape
    cells = (planes, own + 2 * HALO, lanes)
    padded = (planes + 2 * HALO, own + 2 * HALO + 2 * PAD, lanes)
    vmem = pl.BlockSpec(memory_space=pltpu.VMEM)
    f32 = jnp.float32
    return pl.pallas_call(
        lay_kernel,
        in_specs=[vmem] * 4,
        out_specs=[vmem] * 3,
        out_shape=[jax.ShapeDtypeStruct(*x) for x in ((cells, jnp.int32), (padded, f32), (cells, f32))],
        compiler_params=pltpu.CompilerParams(vmem_limit_bytes=16 * MIB),
        cost_estimate=pl.CostEstimate(flops=0, bytes_accessed=LAY_COST, transcendentals=0),
        name="lay",
    )(mesh, old, *beyond)


def own_kernel(
    tables_ref, mesh_x, before_x, bend_x, regions_ref, dopant_ref, rows1_ref, rows2_ref,
    permit_x, dopant_x, electron_x, hole_x, now_x,
):
    planes, own, _ = regions_ref.shape
    slabs = tables_ref.shape[0]
    span = own + 2 * HALO
    up, mid, down = slice(HALO - NEAR, HALO), slice(HALO, HALO + own), slice(HALO + own, HALO + own + NEAR)
    for p in range(planes):
        permit_x[p, mid] = permittivity(regions_ref[p])
        dopant_x[p, mid] = dopant_ref[p]
        for field, field_x in ((0, permit_x), (1, dopant_x)):
            at = 2 * slabs * SUB + (field * planes + p) * NEAR
            field_x[p, up], field_x[p, down] = beside_rows(rows1_ref, rows2_ref, at)
    for slab in range(slabs):
        tables = broadcast_table(tables_ref[slab])

        def some(first, count, _, tables=tables, slab=slab):
            for r in range(0, span, SUB):
                at, rows = PAD + r, slice(r, r + SUB)
                for k in range(count):
                    p = slab * PL + first + k
                    electron_x[p, rows], hole_x[p, rows], now_x[p, rows] = first_sweep(
                        mesh_x[p, rows], tables, before_x[HALO + p, at : at + SUB], bend_x[p, rows],
                        permit_x[p, rows], dopant_x[p, rows], outside_rows(r, span),
                    )
            return _

        grouped(PL, LOOK, some, None)


def own_planes(tables, laid_out, regions, dopant, rows):
    vmem = pl.BlockSpec(memory_space=pltpu.VMEM)
    cells = laid_out[0].shape
    return pl.pallas_call(
        own_kernel,
        in_specs=[vmem] * 8,
        out_specs=[vmem] * 5,
        out_shape=[jax.ShapeDtypeStruct(cells, jnp.float32)] * 5,
        compiler_params=pltpu.CompilerParams(vmem_limit_bytes=16 * MIB),
        cost_estimate=pl.CostEstimate(flops=0, bytes_accessed=LAY_COST, transcendentals=0),
        name="own",
    )(tables, *laid_out, regions, dopant, *rows)


def sweep_kernel(
    packed1_ref, packed2_ref, planes1_ref, planes2_ref, before_x, permit_o, dopant_o, electron_o, hole_o, now_o,
    change_ref, most_ref, permit_x, dopant_x, electron_x, hole_x, now_s, next_s,
):
    _, s, _, ns = position()
    odd_s = (s & 1) == 1
    planes, own, _ = change_ref.shape
    span = own + 2 * HALO
    tops = range(0, span, SUB)

    def bring(first, count, _):
        for k in range(count):
            p = first + k
            q = HALO + p
            for r in tops:
                rows = slice(r, r + SUB)
                permit_x[q, rows] = permit_o[p, rows]
                dopant_x[q, rows] = dopant_o[p, rows]
                electron_x[q, rows] = electron_o[p, rows]
                hole_x[q, rows] = hole_o[p, rows]
                now_s[q, PAD + r : PAD + r + SUB] = now_o[p, rows]
        return _

    grouped(planes, LAY, bring, None)
    for low in (True, False):
        a, b = (packed1_ref, packed2_ref) if low else (packed2_ref, packed1_ref)
        c, d = (planes1_ref, planes2_ref) if low else (planes2_ref, planes1_ref)
        inside = s > 0 if low else s < ns - 1
        top = 2 * NEAR * SUB
        tables = [
            [
                jnp.where(
                    inside,
                    jnp.where(
                        odd_s,
                        jnp.broadcast_to(a[t + g : t + g + 1], (SUB, LANES)),
                        jnp.broadcast_to(b[t + g : t + g + 1], (SUB, LANES)),
                    ),
                    1.0,
                )
                for g in range(SUB)
            ]
            for t in (top, top + SUB)
        ]
        for k in range(NEAR):
            q = 1 + k if low else HALO + planes + k
            for field, field_x in ((0, permit_x), (1, dopant_x)):
                t = (field * NEAR + k) * SUB
                m = (NEAR + HALO) * span + (field * NEAR + k) * own
                field_x[q, :HALO] = jnp.where(odd_s, a[t : t + HALO], b[t : t + HALO])
                field_x[q, HALO : HALO + own] = jnp.where(odd_s, c[m : m + own], d[m : m + own])
                field_x[q, HALO + own :] = jnp.where(odd_s, a[t + HALO : t + SUB], b[t + HALO : t + SUB])
            for r in tops:
                at, rows = PAD + r, slice(r, r + SUB)
                here = slice(k * span + r, k * span + r + SUB)
                permit, dopant = permit_x[q, rows], dopant_x[q, rows]
                choice = jnp.where(odd_s, c[here], d[here]).astype(jnp.int32)
                center = before_x[q, at : at + SUB]
                neighbours = around(
                    center, before_x[q - 1, at : at + SUB], before_x[q + 1, at : at + SUB],
                    before_x[q, at - 1 : at - 1 + SUB], before_x[q, at + 1 : at + 1 + SUB],
                )
                electrons, holes, fresh = first_sweep(
                    choice, tables, center, 6.0 * center - neighbours, permit, dopant, outside_rows(r, span)
                )
                electron_x[q, rows] = electrons
                hole_x[q, rows] = holes
                now_s[q, at : at + SUB] = fresh

    source = now_s
    for sweep in range(1, SWEEPS):
        final = sweep == SWEEPS - 1
        target = next_s if source is now_s else now_s
        starts = range(HALO, HALO + own, SUB) if final else tops

        def step(first, count, most, sweep=sweep, source=source, target=target, starts=starts, final=final):
            for r in starts:
                rows = slice(r, r + SUB)
                at = PAD + r
                rows_b = slice(at, at + SUB)
                held = [source[1 + sweep + first + k, rows_b] for k in range(-1, count + 1)]
                for k in range(count):
                    q = 1 + sweep + first + k
                    center = held[k + 1]
                    neighbours = around(
                        center, held[k], held[k + 2],
                        source[q, at - 1 : at - 1 + SUB], source[q, at + 1 : at + 1 + SUB],
                    )
                    permit = permit_x[q, rows]
                    before = before_x[q, rows_b]
                    moved = center - before
                    electrons = electron_x[q, rows] * jnp.exp(moved)
                    holes = hole_x[q, rows] * jnp.exp(-moved)
                    mismatch = permit * (6.0 * center - neighbours) - (dopant_x[q, rows] + holes - electrons)
                    jacobian = 6.0 * permit + electrons + holes
                    fresh = center - mismatch / jacobian
                    if final:
                        change = fresh - before
                        change_ref[q - HALO, r - HALO : r - HALO + SUB] = change
                        most = jnp.maximum(most, jnp.abs(change))
                    else:
                        target[q, rows_b] = fresh
            return most

        most = grouped(planes + 2 * (SWEEPS - 1 - sweep), BLOCK, step, jnp.zeros((SUB, LANES), jnp.float32))
        if final:
            most_ref[...] = jnp.broadcast_to(jnp.max(most, axis=0, keepdims=True)[None], most_ref.shape)
        source = target


def swept(packed, beyond, fields, own):
    planes, span, lanes = fields[1].shape
    padded = fields[0].shape
    cells = (padded[0], span, lanes)
    vmem = pl.BlockSpec(memory_space=pltpu.VMEM)
    f32 = jnp.float32
    return pl.pallas_call(
        sweep_kernel,
        in_specs=[vmem] * 10,
        out_specs=[vmem, vmem],
        out_shape=[
            jax.ShapeDtypeStruct((planes, own, lanes), f32),
            jax.ShapeDtypeStruct((lax.axis_size(("energy", "space")), 1, lanes), f32),
        ],
        scratch_shapes=[pltpu.VMEM(cells, f32)] * 4 + [pltpu.VMEM(padded, f32)] * 2,
        compiler_params=pltpu.CompilerParams(vmem_limit_bytes=24 * MIB),
        name="sweeps",
    )(*packed, *beyond, *fields)


def write_rows(out_ref, result, sems, old_ref, parts, masks, scale):
    e = lax.axis_index("energy")
    planes, own, _ = parts[0].shape
    size = planes // SETTLE
    copies = []
    for b in range(SETTLE):
        at = slice(b * size, (b + 1) * size)
        for k, (mask, part) in enumerate(zip(masks, parts)):
            rows = pl.ds(pl.multiple_of((e ^ mask) * own, SUB), own)
            result[k, at] = old_ref[at, rows] + part[at] * scale
            copies.append(pltpu.make_async_copy(result.at[k, at], out_ref.at[at, rows], sems.at[b, k]))
            copies[-1].start()
    for copy in copies:
        copy.wait()


def settle_kernel(most_ref, old_ref, *rest, masks):
    parts, (out_ref, scale_ref, result, sems) = rest[:-4], rest[-4:]
    scale = 1.0 / (1.0 + jnp.max(most_ref[...]))
    scale_ref[...] = jnp.full(scale_ref.shape, scale)
    write_rows(out_ref, result, sems, old_ref, parts, masks, scale)


def settle_more_kernel(scale_ref, old_ref, *rest, masks):
    parts, (_, out_ref, result, sems) = rest[:-4], rest[-4:]
    write_rows(out_ref, result, sems, old_ref, parts, masks, scale_ref[0:1][None])


def settled(most, old, parts, late):
    vmem, anywhere = pl.BlockSpec(memory_space=pltpu.VMEM), pl.BlockSpec(memory_space=pl.ANY)
    whole = jax.ShapeDtypeStruct(old.shape, jnp.float32)

    def scratch(count):
        return [
            pltpu.VMEM((count,) + parts[0].shape, jnp.float32),
            pltpu.SemaphoreType.DMA((SETTLE, count)),
        ]

    out, scale = pl.pallas_call(
        functools.partial(settle_kernel, masks=tuple(parts)),
        in_specs=[vmem] * (2 + len(parts)),
        out_specs=[anywhere, vmem],
        out_shape=[whole, jax.ShapeDtypeStruct((SUB, LANES), jnp.float32)],
        scratch_shapes=scratch(len(parts)),
        compiler_params=pltpu.CompilerParams(vmem_limit_bytes=16 * MIB),
        cost_estimate=pl.CostEstimate(flops=0, bytes_accessed=LAY_COST, transcendentals=0),
        name="settle",
    )(most, old, *parts.values())
    return pl.pallas_call(
        functools.partial(settle_more_kernel, masks=tuple(late)),
        in_specs=[vmem] * (2 + len(late)) + [anywhere],
        out_specs=anywhere,
        out_shape=whole,
        input_output_aliases={2 + len(late): 0},
        scratch_shapes=scratch(len(late)),
        compiler_params=pltpu.CompilerParams(vmem_limit_bytes=16 * MIB),
        name="settle_more",
    )(scale, old, *late.values(), out)


def pairs(axis, odd_first):
    count = lax.axis_size(axis)
    out = []
    for low in range(1 if odd_first else 0, count - 1, 2):
        out += [(low, low + 1), (low + 1, low)]
    return out


def toggled(x, axis, mask):
    return lax.ppermute(x, axis, [(i, i ^ mask) for i in range(lax.axis_size(axis))])


def on_device(green_blocks, injection, mesh_state_choice, regions, dopant_charge_field, earlier_voltage):
    ne = lax.axis_size("energy")
    own = regions.shape[1]
    green, inject = green_blocks[0], injection[0]

    def exchanged(sent, axis):
        return [lax.ppermute(x, axis, pairs(axis, odd_first)) for x, odd_first in zip(sent, (False, True))]

    rows, beyond = edges(regions, dopant_charge_field, mesh_state_choice, earlier_voltage, green, inject)
    beyond = exchanged(beyond, "space")
    tables, packed1, packed2 = orbital_table(green, inject, rows)
    alone, beyond = lax.optimization_barrier((tables, beyond))
    second = [k for k in range(3, ne) if k & (k + 1) == 0]
    terms = [tables]
    for k in range(1, ne):
        sent = packed1 if k == 1 else packed2 if k in second else alone
        terms.append(toggled(sent, "energy", k))
    e = lax.axis_index("energy")
    partner = jnp.where(e & 1 == 1, e + 1, e - 1)
    rows = [terms[1], terms[3]]
    for k in second[1:]:
        rows[1] = jnp.where(e ^ partner == k, terms[k], rows[1])
    laid_out = laid(mesh_state_choice, earlier_voltage, beyond, own)
    terms, laid_out = lax.optimization_barrier((terms, laid_out))
    tables, packed = joined(terms, rows)
    packed = exchanged(packed, "space")
    fields = own_planes(tables, laid_out, regions, dopant_charge_field, rows)
    change, most = swept(packed, beyond, (laid_out[1], *fields), own)
    parts, late = {0: change}, {}
    for k in range(2, ne, 2):
        parts[k] = toggled(change, "energy", k)
    parts[1] = toggled(change, "energy", 1)
    most = lax.all_to_all(most, ("energy", "space"), 0, 0)
    far = [parts[k] for k in range(2, ne, 2)]
    most, far = lax.optimization_barrier((most, far))
    for k, part in zip(range(2, ne, 2), far):
        late[k ^ 1] = toggled(part, "energy", 1)
    return settled(most, earlier_voltage, parts, late)


def solution(mesh):
    placed = (
        P("energy", "space", None, None, None),
        P("energy", "space", None, None),
        P("space", None, None),
        P("space", "energy", None),
        P("space", "energy", None),
        P("space", None, None),
    )
    return jax.shard_map(
        on_device, mesh=mesh, in_specs=placed, out_specs=P("space", None, None), check_vma=False
    )
```

```python
import functools

import jax
import jax.numpy as jnp
from jax import lax
from jax.experimental import pallas as pl
from jax.experimental.pallas import tpu as pltpu
from jax.sharding import PartitionSpec as P

PL = 16
SWEEPS = 4
HALO = 4
PAD = 8
LANES = 128
SUB = 8
MIB = 1 << 20
BLOCK = 32
LOOK = 16
LAY = 16
SETTLE = 2
EDGE_COST = 10 * MIB
TABLE_COST = 10 * MIB
LAY_COST = 3 * MIB
LATER = pl.ANY
PAIRS = 64


def merge(parts, width):
    lane = lax.broadcasted_iota(jnp.int32, (SUB, LANES), 1)
    while len(parts) > 1:
        low = (lane & width) == 0
        merged = []
        for a, b in zip(parts[::2], parts[1::2]):
            merged.append(jnp.where(low, a, b) + pltpu.roll(jnp.where(low, b, a), width, 1))
        parts = merged
        width *= 2
    return parts[0]


def table_kernel(green_ref, inject_ref, rows1_ref, rows2_ref, out_ref, packed1_ref, packed2_ref, part_ref):
    slabs, _, states, columns = green_ref.shape
    chunks = columns // LANES
    groups = states // SUB
    for packed_ref, rows_ref in ((packed1_ref, rows1_ref), (packed2_ref, rows2_ref)):
        packed_ref[2 * slabs * SUB :] = rows_ref[...]
    for slab in range(slabs):
        weights = [
            [
                jnp.broadcast_to(inject_ref[slab, c : c + 1, k * LANES : (k + 1) * LANES], (SUB, LANES))
                for k in range(chunks)
            ]
            for c in range(2)
        ]

        def some_groups(i, _, slab=slab, weights=weights):
            for pair in range(PAIRS):
                sums = [[], []]
                for g in range(2):
                    rows = pl.ds(pl.multiple_of((i * (2 * PAIRS) + 2 * pair + g) * SUB, SUB), SUB)
                    total = [None, None]
                    for k in range(chunks):
                        cols = slice(k * LANES, (k + 1) * LANES)
                        re = green_ref[slab, 0, rows, cols]
                        im = green_ref[slab, 1, rows, cols]
                        squared = re * re + im * im
                        for c in range(2):
                            term = squared * weights[c][k]
                            total[c] = term if total[c] is None else total[c] + term
                    for c in range(2):
                        sums[c].append(total[c])
                for c in range(2):
                    part_ref[slab, c, i * PAIRS + pair] = merge(sums[c], 1)
            return _

        lax.fori_loop(0, groups // (2 * PAIRS), some_groups, None)
    lane = lax.broadcasted_iota(jnp.int32, (SUB, LANES), 1)
    count, width = groups // 2, 2
    while count > 1:
        low = (lane & width) == 0
        count //= 2
        for slab in range(slabs):
            for c in range(2):
                for k in range(count):
                    a, b = part_ref[slab, c, 2 * k], part_ref[slab, c, 2 * k + 1]
                    both = jnp.where(low, a, b) + pltpu.roll(jnp.where(low, b, a), width, 1)
                    if count > 1:
                        part_ref[slab, c, k] = both
                    else:
                        out_ref[slab, c] = both
                        at = (2 * slab + c) * SUB
                        packed1_ref[at : at + SUB] = both
                        packed2_ref[at : at + SUB] = both
        width *= 2


def orbital_table(green, inject, rows):
    slabs, _, states, _ = green.shape
    vmem = pl.BlockSpec(memory_space=pltpu.VMEM)
    packed = jax.ShapeDtypeStruct((2 * slabs * SUB + rows[0].shape[0], LANES), jnp.float32)
    return pl.pallas_call(
        table_kernel,
        in_specs=[vmem] * 4,
        out_specs=[vmem] * 3,
        out_shape=[jax.ShapeDtypeStruct((slabs, 2, SUB, LANES), jnp.float32), packed, packed],
        scratch_shapes=[pltpu.VMEM((slabs, 2, states // SUB // 2, SUB, LANES), jnp.float32)],
        compiler_params=pltpu.CompilerParams(vmem_limit_bytes=20 * MIB),
        cost_estimate=pl.CostEstimate(flops=0, bytes_accessed=TABLE_COST, transcendentals=0),
        name="table",
    )(green, inject, *rows)


def lookup(tables, choice):
    lane = choice >> 3
    group = choice & (SUB - 1)
    bits = [(group & (1 << b)) != 0 for b in range(3)]
    out = []
    for table in tables:
        found = [jnp.take_along_axis(t, lane, axis=1, mode="promise_in_bounds") for t in table]
        for bit in bits:
            found = [jnp.where(bit, found[2 * k + 1], found[2 * k]) for k in range(len(found) // 2)]
        out.append(found[0])
    return out


def permittivity(regions):
    return jnp.where(regions == 0, 1.0, jnp.where(regions == 1, 0.33, 1.7)).astype(jnp.float32)


def grouped(count, size, step, carry):
    odd = count % size
    if odd:
        carry = step(0, odd, carry)
    if count // size < 2:
        return step(odd, size, carry) if count >= size else carry
    return lax.fori_loop(0, count // size, lambda i, c: step(odd + i * size, size, c), carry)


def around(center, below, above, left, right):
    lane = lax.broadcasted_iota(jnp.int32, (SUB, LANES), 1)
    after = jnp.where(lane < LANES - 1, pltpu.roll(center, LANES - 1, 1), 0.0)
    ahead = jnp.where(lane > 0, pltpu.roll(center, 1, 1), 0.0)
    return above + below + right + left + after + ahead


def position():
    return lax.axis_index("energy"), lax.axis_index("space"), lax.axis_size("energy"), lax.axis_size("space")


NEAR = HALO - 1


def edge_kernel(
    regions_ref, dopant_ref, mesh_ref, old_ref, green_ref, inject_ref,
    rows1_ref, rows2_ref, planes1_ref, planes2_ref,
    regions_s, dopant_s, mesh_s, old_s, sems,
):
    e, s, ne, _ = position()
    odd_e, odd_s = (e & 1) == 1, (s & 1) == 1
    planes, own, _ = regions_s.shape
    pieces = [(regions_ref, regions_s), (dopant_ref, dopant_s)]
    for source, held in ((mesh_ref, mesh_s), (old_ref, old_s)):
        pieces.append((source.at[0:HALO], held.at[0]))
        pieces.append((source.at[planes - HALO : planes], held.at[1]))
    copies = [pltpu.make_async_copy(a, b, sems.at[k]) for k, (a, b) in enumerate(pieces)]
    for copy in copies:
        copy.start()
    for copy in copies[:2]:
        copy.wait()
    top, bottom = slice(0, NEAR), slice(own - NEAR, own)
    for p in range(planes):
        for field, values in ((0, permittivity(regions_s[p])), (1, dopant_s[p])):
            at = (field * planes + p) * NEAR
            rows1_ref[at : at + NEAR] = jnp.where(odd_e, values[top], values[bottom])
            rows2_ref[at : at + NEAR] = jnp.where(odd_e, values[bottom], values[top])
    for copy in copies[2:]:
        copy.wait()
    row0 = pl.multiple_of(e * own, SUB)
    up_from = pl.multiple_of(jnp.maximum(row0 - SUB, 0), SUB)
    down_from = pl.multiple_of(jnp.minimum(row0 + own, mesh_s.shape[2] - SUB), SUB)
    span = own + 2 * HALO
    for out_ref, side in ((planes1_ref, jnp.where(odd_s, 0, 1)), (planes2_ref, jnp.where(odd_s, 1, 0))):
        for k in range(NEAR):
            p, at = k + side, k * span
            out_ref[at : at + HALO] = mesh_s[side, p, pl.ds(up_from, SUB)][SUB - HALO :].astype(jnp.float32)
            out_ref[at + HALO : at + HALO + own] = mesh_s[side, p, pl.ds(row0, own)].astype(jnp.float32)
            out_ref[at + HALO + own : at + span] = mesh_s[side, p, pl.ds(down_from, SUB)][:HALO].astype(jnp.float32)
            low = planes - NEAR + k
            for field, at in ((0, (NEAR + HALO) * span + k * own), (1, (NEAR + HALO) * span + (NEAR + k) * own)):
                held = regions_s if field == 0 else dopant_s
                values = jnp.where(side == 0, held[k], held[low])
                out_ref[at : at + own] = permittivity(values) if field == 0 else values
        for k in range(HALO):
            at = (NEAR + k) * span
            out_ref[at : at + HALO] = jnp.where(e > 0, old_s[side, k, pl.ds(up_from, SUB)][SUB - HALO :], 0.0)
            out_ref[at + HALO : at + HALO + own] = old_s[side, k, pl.ds(row0, own)]
            out_ref[at + HALO + own : at + span] = jnp.where(
                e < ne - 1, old_s[side, k, pl.ds(down_from, SUB)][:HALO], 0.0
            )


def edges(regions, dopant, mesh, old, green, inject):
    planes, own, lanes = regions.shape
    rows = jax.ShapeDtypeStruct((2 * NEAR * planes, lanes), jnp.float32)
    cells = jax.ShapeDtypeStruct(((NEAR + HALO) * (own + 2 * HALO) + 2 * NEAR * own, lanes), jnp.float32)
    held = (2, HALO) + mesh.shape[1:]
    outs = pl.pallas_call(
        edge_kernel,
        in_specs=[pl.BlockSpec(memory_space=pl.ANY)] * 6,
        out_specs=[pl.BlockSpec(memory_space=pltpu.VMEM)] * 4,
        out_shape=[rows, rows, cells, cells],
        scratch_shapes=[
            pltpu.VMEM(regions.shape, jnp.int32),
            pltpu.VMEM(regions.shape, jnp.float32),
            pltpu.VMEM(held, jnp.int32),
            pltpu.VMEM(held, jnp.float32),
            pltpu.SemaphoreType.DMA((6,)),
        ],
        compiler_params=pltpu.CompilerParams(vmem_limit_bytes=8 * MIB),
        cost_estimate=pl.CostEstimate(flops=0, bytes_accessed=EDGE_COST, transcendentals=0),
        name="edges",
    )(*(pltpu.with_memory_space_constraint(x, pltpu.HBM) for x in (regions, dopant, mesh, old, green, inject)))
    return outs[:2], outs[2:]


def beside_rows(rows1_ref, rows2_ref, at):
    e, _, ne, _ = position()
    odd = (e & 1) == 1
    one = rows1_ref[at : at + NEAR]
    two = jnp.where((e > 0) & (e < ne - 1), rows2_ref[at : at + NEAR], 0.0)
    return jnp.where(odd, one, two), jnp.where(odd, two, one)


def join_kernel(*refs):
    rows1_ref, rows2_ref = refs[-5:-3]
    tables_ref, first_ref, second_ref = refs[-3:]
    odd_s = (lax.axis_index("space") & 1) == 1
    slabs = tables_ref.shape[0]
    ahead = 2 * slabs * SUB
    planes = (rows1_ref.shape[0] - ahead) // (2 * NEAR)
    tables = []
    for slab in range(slabs):
        for c in range(2):
            at = (2 * slab + c) * SUB
            terms = [ref[slab, c] if len(ref.shape) == 4 else ref[at : at + SUB] for ref in refs[:-5]]
            while len(terms) > 1:
                terms = [a + b for a, b in zip(terms[::2], terms[1::2])]
            tables_ref[slab, c] = terms[0]
            tables.append(terms[0])
    for k in range(NEAR):
        for field in range(2):
            low = beside_rows(rows1_ref, rows2_ref, ahead + (field * planes + k) * NEAR)
            high = beside_rows(rows1_ref, rows2_ref, ahead + (field * planes + planes - NEAR + k) * NEAR)
            top = (field * NEAR + k) * SUB
            for at, a, b in zip((top + 1, top + HALO), low, high):
                first_ref[at : at + NEAR] = jnp.where(odd_s, a, b)
                second_ref[at : at + NEAR] = jnp.where(odd_s, b, a)
    for c in range(2):
        top = (2 * NEAR + c) * SUB
        low, high = tables[c], tables[2 * (slabs - 1) + c]
        first_ref[top : top + SUB] = jnp.where(odd_s, low, high)
        second_ref[top : top + SUB] = jnp.where(odd_s, high, low)


def joined(terms, rows):
    vmem = pl.BlockSpec(memory_space=pltpu.VMEM)
    packed = jax.ShapeDtypeStruct((2 * (NEAR + 1) * SUB, LANES), jnp.float32)
    outs = pl.pallas_call(
        join_kernel,
        in_specs=[vmem] * (len(terms) + 2),
        out_specs=[vmem] * 3,
        out_shape=[jax.ShapeDtypeStruct(terms[0].shape, jnp.float32), packed, packed],
        compiler_params=pltpu.CompilerParams(vmem_limit_bytes=8 * MIB),
        name="join",
    )(*terms, *rows)
    return outs[0], outs[1:]


def broadcast_table(slab_value):
    return [[jnp.broadcast_to(slab_value[c, g : g + 1], (SUB, LANES)) for g in range(SUB)] for c in range(2)]


def first_sweep(choice, tables, center, bend, permit, dopant, outside):
    electrons, holes = lookup(tables, choice)
    if outside is not None:
        electrons, holes = jnp.where(outside, 1.0, electrons), jnp.where(outside, 1.0, holes)
    mismatch = permit * bend - (dopant + holes - electrons)
    jacobian = 6.0 * permit + electrons + holes
    return electrons, holes, center - mismatch / jacobian


def outside_rows(r, span):
    e, _, ne, _ = position()
    row = lax.broadcasted_iota(jnp.int32, (SUB, LANES), 0)
    outside = None
    if r == 0:
        outside = (row < HALO) & (e == 0)
    if r == span - SUB:
        below = (row >= SUB - HALO) & (e == ne - 1)
        outside = below if outside is None else outside | below
    return outside


def lay_kernel(mesh_ref, old_ref, planes1_ref, planes2_ref, mesh_x, before_x, bend_x):
    e, s, ne, _ = position()
    odd_s = (s & 1) == 1
    planes, span, _ = mesh_x.shape
    own = span - 2 * HALO
    row0 = pl.multiple_of(e * own, SUB)
    up, mid, down = slice(0, HALO), slice(HALO, HALO + own), slice(HALO + own, span)
    up_b, mid_b, down_b = (slice(PAD + x.start, PAD + x.stop) for x in (up, mid, down))
    up_from = pl.multiple_of(jnp.maximum(row0 - SUB, 0), SUB)
    down_from = pl.multiple_of(jnp.minimum(row0 + own, mesh_ref.shape[1] - SUB), SUB)

    def lay(first, count, _):
        for k in range(count):
            p = first + k
            q = p + HALO
            mesh_x[p, mid] = mesh_ref[p, pl.ds(row0, own)]
            mesh_x[p, up] = mesh_ref[p, pl.ds(up_from, SUB)][SUB - HALO :]
            mesh_x[p, down] = mesh_ref[p, pl.ds(down_from, SUB)][:HALO]
            before_x[q, mid_b] = old_ref[p, pl.ds(row0, own)]
            before_x[q, up_b] = jnp.where(e > 0, old_ref[p, pl.ds(up_from, SUB)][SUB - HALO :], 0.0)
            before_x[q, down_b] = jnp.where(e < ne - 1, old_ref[p, pl.ds(down_from, SUB)][:HALO], 0.0)
        return _

    grouped(planes, LAY, lay, None)
    for k in range(HALO):
        at = (NEAR + k) * span
        a, b = planes1_ref[at : at + span], planes2_ref[at : at + span]
        before_x[k, PAD : PAD + span] = jnp.where(odd_s, a, b)
        before_x[HALO + planes + k, PAD : PAD + span] = jnp.where(odd_s, b, a)

    def bends(first, count, _):
        for r in range(0, span, SUB):
            at = PAD + r
            held = [before_x[HALO + first + k, at : at + SUB] for k in range(-1, count + 1)]
            for k in range(count):
                q = HALO + first + k
                neighbours = around(
                    held[k + 1], held[k], held[k + 2],
                    before_x[q, at - 1 : at - 1 + SUB], before_x[q, at + 1 : at + 1 + SUB],
                )
                bend_x[first + k, r : r + SUB] = 6.0 * held[k + 1] - neighbours
        return _

    grouped(planes, BLOCK, bends, None)


def laid(mesh, old, beyond, own):
    planes, _, lanes = mesh.shape
    cells = (planes, own + 2 * HALO, lanes)
    padded = (planes + 2 * HALO, own + 2 * HALO + 2 * PAD, lanes)
    vmem = pl.BlockSpec(memory_space=pltpu.VMEM)
    f32 = jnp.float32
    return pl.pallas_call(
        lay_kernel,
        in_specs=[vmem] * 4,
        out_specs=[vmem] * 3,
        out_shape=[jax.ShapeDtypeStruct(*x) for x in ((cells, jnp.int32), (padded, f32), (cells, f32))],
        compiler_params=pltpu.CompilerParams(vmem_limit_bytes=16 * MIB),
        cost_estimate=pl.CostEstimate(flops=0, bytes_accessed=LAY_COST, transcendentals=0),
        name="lay",
    )(mesh, old, *beyond)


def later_sweep(center, below, above, left, right, before, permit, dopant, electrons, holes):
    moved = center - before
    electrons = electrons * jnp.exp(moved)
    holes = holes * jnp.exp(-moved)
    bend = 6.0 * center - around(center, below, above, left, right)
    mismatch = permit * bend - (dopant + holes - electrons)
    jacobian = 6.0 * permit + electrons + holes
    return center - mismatch / jacobian


def own_kernel(
    tables_ref, mesh_x, before_x, bend_x, regions_ref, dopant_ref, rows1_ref, rows2_ref,
    permit_x, dopant_x, electron_x, hole_x, change_x, most_x, *level_x,
):
    planes, own, _ = regions_ref.shape
    slabs = tables_ref.shape[0]
    span = own + 2 * HALO
    up, mid, down = slice(HALO - NEAR, HALO), slice(HALO, HALO + own), slice(HALO + own, HALO + own + NEAR)
    for p in range(planes):
        permit_x[p, mid] = permittivity(regions_ref[p])
        dopant_x[p, mid] = dopant_ref[p]
        for field, field_x in ((0, permit_x), (1, dopant_x)):
            at = 2 * slabs * SUB + (field * planes + p) * NEAR
            field_x[p, up], field_x[p, down] = beside_rows(rows1_ref, rows2_ref, at)
    for slab in range(slabs):
        tables = broadcast_table(tables_ref[slab])

        def some(first, count, _, tables=tables, slab=slab):
            for r in range(0, span, SUB):
                at, rows = PAD + r, slice(r, r + SUB)
                for k in range(count):
                    p = slab * PL + first + k
                    electron_x[p, rows], hole_x[p, rows], level_x[0][p, at : at + SUB] = first_sweep(
                        mesh_x[p, rows], tables, before_x[HALO + p, at : at + SUB], bend_x[p, rows],
                        permit_x[p, rows], dopant_x[p, rows], outside_rows(r, span),
                    )
            return _

        grouped(PL, LOOK, some, None)


    for sweep in range(1, SWEEPS):
        final = sweep == SWEEPS - 1
        starts = range(HALO, HALO + own, SUB) if final else range(0, span, SUB)

        def step(first, count, most, sweep=sweep, starts=starts, final=final):
            source = level_x[sweep - 1]
            for r in starts:
                rows = slice(r, r + SUB)
                at = PAD + r
                held = [source[sweep + first + k, at : at + SUB] for k in range(-1, count + 1)]
                for k in range(count):
                    p = sweep + first + k
                    before = before_x[HALO + p, at : at + SUB]
                    fresh = later_sweep(
                        held[k + 1], held[k], held[k + 2],
                        source[p, at - 1 : at - 1 + SUB], source[p, at + 1 : at + 1 + SUB],
                        before, permit_x[p, rows], dopant_x[p, rows], electron_x[p, rows], hole_x[p, rows],
                    )
                    if final:
                        change_x[p, r - HALO : r - HALO + SUB] = fresh - before
                        most = jnp.maximum(most, jnp.abs(fresh - before))
                    else:
                        level_x[sweep][p, at : at + SUB] = fresh
            return most

        most = grouped(planes - 2 * sweep, BLOCK, step, jnp.zeros((SUB, LANES), jnp.float32))
        if final:
            most_x[...] = most


def own_planes(tables, laid_out, regions, dopant, rows):
    vmem = pl.BlockSpec(memory_space=pltpu.VMEM)
    cells = laid_out[0].shape
    padded = (cells[0],) + laid_out[1].shape[1:]
    shapes = [cells] * 4 + [regions.shape, (SUB, LANES)] + [padded] * (SWEEPS - 1)
    return pl.pallas_call(
        own_kernel,
        in_specs=[vmem] * 8,
        out_specs=[vmem] * len(shapes),
        out_shape=[jax.ShapeDtypeStruct(shape, jnp.float32) for shape in shapes],
        compiler_params=pltpu.CompilerParams(vmem_limit_bytes=24 * MIB),
        cost_estimate=pl.CostEstimate(flops=0, bytes_accessed=LAY_COST, transcendentals=0),
        name="own",
    )(tables, *laid_out, regions, dopant, *rows)


def sweep_kernel(
    packed1_ref, packed2_ref, planes1_ref, planes2_ref, before_x, permit_o, dopant_o, electron_o, hole_o, change_o,
    most_o, level1_o, level2_o, level3_o, change_ref, most_ref, permit_s, dopant_s, electron_s, hole_s, level_s,
):
    _, s, _, ns = position()
    odd_s = (s & 1) == 1
    planes, own, _ = change_ref.shape
    span = own + 2 * HALO
    tops = range(0, span, SUB)
    levels_o = (level1_o, level2_o, level3_o)

    def plane_of(end, j):
        return j if end == 0 else planes + 2 * HALO - 1 - j

    for end in range(2):
        a, b = (packed1_ref, packed2_ref) if end == 0 else (packed2_ref, packed1_ref)
        c, d = (planes1_ref, planes2_ref) if end == 0 else (planes2_ref, planes1_ref)
        inside = s > 0 if end == 0 else s < ns - 1
        top = 2 * NEAR * SUB
        tables = [
            [
                jnp.where(
                    inside,
                    jnp.where(
                        odd_s,
                        jnp.broadcast_to(a[t + g : t + g + 1], (SUB, LANES)),
                        jnp.broadcast_to(b[t + g : t + g + 1], (SUB, LANES)),
                    ),
                    1.0,
                )
                for g in range(SUB)
            ]
            for t in (top, top + SUB)
        ]
        for j in range(1, HALO):
            q = plane_of(end, j)
            k = j - 1 if end == 0 else NEAR - j
            for field, field_s in ((0, permit_s), (1, dopant_s)):
                t = (field * NEAR + k) * SUB
                m = (NEAR + HALO) * span + (field * NEAR + k) * own
                field_s[end, j, :HALO] = jnp.where(odd_s, a[t : t + HALO], b[t : t + HALO])
                field_s[end, j, HALO : HALO + own] = jnp.where(odd_s, c[m : m + own], d[m : m + own])
                field_s[end, j, HALO + own :] = jnp.where(odd_s, a[t + HALO : t + SUB], b[t + HALO : t + SUB])
            for r in tops:
                at, rows = PAD + r, slice(r, r + SUB)
                here = slice(k * span + r, k * span + r + SUB)
                choice = jnp.where(odd_s, c[here], d[here]).astype(jnp.int32)
                center = before_x[q, at : at + SUB]
                neighbours = around(
                    center, before_x[q - 1, at : at + SUB], before_x[q + 1, at : at + SUB],
                    before_x[q, at - 1 : at - 1 + SUB], before_x[q, at + 1 : at + 1 + SUB],
                )
                electron_s[end, j, rows], hole_s[end, j, rows], level_s[end, 0, j, at : at + SUB] = first_sweep(
                    choice, tables, center, 6.0 * center - neighbours,
                    permit_s[end, j, rows], dopant_s[end, j, rows], outside_rows(r, span),
                )
        for sweep in range(1, SWEEPS):
            for j in (HALO + sweep - 1, HALO + sweep):
                p = plane_of(end, j) - HALO
                level_s[end, sweep - 1, j] = levels_o[sweep - 1][p]
    for p in range(SWEEPS - 1, planes - SWEEPS + 1):
        change_ref[p] = change_o[p]

    most = most_o[...]
    for sweep in range(1, SWEEPS):
        final = sweep == SWEEPS - 1
        for end in range(2):
            source = level_s.at[end, sweep - 1]
            for r in range(HALO, HALO + own, SUB) if final else tops:
                at, rows = PAD + r, slice(r, r + SUB)
                for j in range(1 + sweep, HALO + sweep):
                    q = plane_of(end, j)
                    p = q - HALO
                    if j < HALO:
                        fields = [ref[end, j, rows] for ref in (permit_s, dopant_s, electron_s, hole_s)]
                    else:
                        fields = [ref[p, rows] for ref in (permit_o, dopant_o, electron_o, hole_o)]
                    before = before_x[q, at : at + SUB]
                    fresh = later_sweep(
                        source[j, at : at + SUB], source[j - 1, at : at + SUB], source[j + 1, at : at + SUB],
                        source[j, at - 1 : at - 1 + SUB], source[j, at + 1 : at + 1 + SUB], before, *fields,
                    )
                    if final:
                        change_ref[p, r - HALO : r - HALO + SUB] = fresh - before
                        most = jnp.maximum(most, jnp.abs(fresh - before))
                    else:
                        level_s[end, sweep, j, at : at + SUB] = fresh
    most_ref[...] = jnp.broadcast_to(jnp.max(most, axis=0, keepdims=True)[None], most_ref.shape)


def swept(packed, beyond, fields, own):
    planes, span, lanes = fields[1].shape
    height = fields[0].shape[1]
    vmem = pl.BlockSpec(memory_space=pltpu.VMEM)
    f32 = jnp.float32
    return pl.pallas_call(
        sweep_kernel,
        in_specs=[vmem] * (4 + len(fields)),
        out_specs=[vmem, vmem],
        out_shape=[
            jax.ShapeDtypeStruct((planes, own, lanes), f32),
            jax.ShapeDtypeStruct((lax.axis_size(("energy", "space")), 1, lanes), f32),
        ],
        scratch_shapes=[pltpu.VMEM((2, HALO, span, lanes), f32)] * 4
        + [pltpu.VMEM((2, SWEEPS - 1, 2 * HALO, height, lanes), f32)],
        compiler_params=pltpu.CompilerParams(vmem_limit_bytes=24 * MIB),
        name="sweeps",
    )(*packed, *beyond, *fields)


def write_rows(out_ref, result, sems, old_ref, parts, masks, scale):
    e = lax.axis_index("energy")
    planes, own, _ = parts[0].shape
    size = planes // SETTLE
    copies = []
    for b in range(SETTLE):
        at = slice(b * size, (b + 1) * size)
        for k, (mask, part) in enumerate(zip(masks, parts)):
            rows = pl.ds(pl.multiple_of((e ^ mask) * own, SUB), own)
            result[k, at] = old_ref[at, rows] + part[at] * scale
            copies.append(pltpu.make_async_copy(result.at[k, at], out_ref.at[at, rows], sems.at[b, k]))
            copies[-1].start()
    for copy in copies:
        copy.wait()


def settle_kernel(most_ref, old_ref, *rest, masks):
    parts, (out_ref, scale_ref, result, sems) = rest[:-4], rest[-4:]
    scale = 1.0 / (1.0 + jnp.max(most_ref[...]))
    scale_ref[...] = jnp.full(scale_ref.shape, scale)
    write_rows(out_ref, result, sems, old_ref, parts, masks, scale)


def settle_more_kernel(scale_ref, old_ref, *rest, masks):
    parts, (_, out_ref, result, sems) = rest[:-4], rest[-4:]
    write_rows(out_ref, result, sems, old_ref, parts, masks, scale_ref[0:1][None])


def settled(most, old, parts, late):
    vmem, anywhere = pl.BlockSpec(memory_space=pltpu.VMEM), pl.BlockSpec(memory_space=pl.ANY)
    whole = jax.ShapeDtypeStruct(old.shape, jnp.float32)

    def scratch(count):
        return [
            pltpu.VMEM((count,) + parts[0].shape, jnp.float32),
            pltpu.SemaphoreType.DMA((SETTLE, count)),
        ]

    out, scale = pl.pallas_call(
        functools.partial(settle_kernel, masks=tuple(parts)),
        in_specs=[vmem] * (2 + len(parts)),
        out_specs=[anywhere, vmem],
        out_shape=[whole, jax.ShapeDtypeStruct((SUB, LANES), jnp.float32)],
        scratch_shapes=scratch(len(parts)),
        compiler_params=pltpu.CompilerParams(vmem_limit_bytes=16 * MIB),
        cost_estimate=pl.CostEstimate(flops=0, bytes_accessed=LAY_COST, transcendentals=0),
        name="settle",
    )(most, old, *parts.values())
    return pl.pallas_call(
        functools.partial(settle_more_kernel, masks=tuple(late)),
        in_specs=[vmem] * (2 + len(late)) + [anywhere],
        out_specs=anywhere,
        out_shape=whole,
        input_output_aliases={2 + len(late): 0},
        scratch_shapes=scratch(len(late)),
        compiler_params=pltpu.CompilerParams(vmem_limit_bytes=16 * MIB),
        name="settle_more",
    )(scale, old, *late.values(), out)


def pairs(axis, odd_first):
    count = lax.axis_size(axis)
    out = []
    for low in range(1 if odd_first else 0, count - 1, 2):
        out += [(low, low + 1), (low + 1, low)]
    return out


def toggled(x, axis, mask):
    return lax.ppermute(x, axis, [(i, i ^ mask) for i in range(lax.axis_size(axis))])


def on_device(green_blocks, injection, mesh_state_choice, regions, dopant_charge_field, earlier_voltage):
    ne = lax.axis_size("energy")
    own = regions.shape[1]
    green, inject = green_blocks[0], injection[0]

    def exchanged(sent, axis):
        return [lax.ppermute(x, axis, pairs(axis, odd_first)) for x, odd_first in zip(sent, (False, True))]

    rows, beyond = edges(regions, dopant_charge_field, mesh_state_choice, earlier_voltage, green, inject)
    beyond = exchanged(beyond, "space")
    tables, packed1, packed2 = orbital_table(green, inject, rows)
    alone, beyond = lax.optimization_barrier((tables, beyond))
    second = [k for k in range(3, ne) if k & (k + 1) == 0]
    terms = [tables]
    for k in range(1, ne):
        sent = packed1 if k == 1 else packed2 if k in second else alone
        terms.append(toggled(sent, "energy", k))
    e = lax.axis_index("energy")
    partner = jnp.where(e & 1 == 1, e + 1, e - 1)
    rows = [terms[1], terms[3]]
    for k in second[1:]:
        rows[1] = jnp.where(e ^ partner == k, terms[k], rows[1])
    laid_out = laid(mesh_state_choice, earlier_voltage, beyond, own)
    terms, laid_out = lax.optimization_barrier((terms, laid_out))
    tables, packed = joined(terms, rows)
    packed = exchanged(packed, "space")
    fields = own_planes(tables, laid_out, regions, dopant_charge_field, rows)
    change, most = swept(packed, beyond, (laid_out[1], *fields), own)
    parts, late = {0: change}, {}
    for k in range(2, ne, 2):
        parts[k] = toggled(change, "energy", k)
    parts[1] = toggled(change, "energy", 1)
    most = lax.all_to_all(most, ("energy", "space"), 0, 0)
    far = [parts[k] for k in range(2, ne, 2)]
    most, far = lax.optimization_barrier((most, far))
    for k, part in zip(range(2, ne, 2), far):
        late[k ^ 1] = toggled(part, "energy", 1)
    return settled(most, earlier_voltage, parts, late)


def solution(mesh):
    placed = (
        P("energy", "space", None, None, None),
        P("energy", "space", None, None),
        P("space", None, None),
        P("space", "energy", None),
        P("space", "energy", None),
        P("space", None, None),
    )
    return jax.shard_map(
        on_device, mesh=mesh, in_specs=placed, out_specs=P("space", None, None), check_vma=False
    )
```

```python
import functools

import jax
import jax.numpy as jnp
from jax import lax
from jax.experimental import pallas as pl
from jax.experimental.pallas import tpu as pltpu
from jax.sharding import PartitionSpec as P

PL = 16
SWEEPS = 4
HALO = 4
PAD = 8
LANES = 128
SUB = 8
MIB = 1 << 20
BLOCK = 32
LOOK = 16
LAY = 16
SETTLE = 2
EDGE_COST = 10 * MIB
TABLE_COST = 10 * MIB
LAY_COST = 3 * MIB
LATER = pl.ANY
PAIRS = 64


def merge(parts, width):
    lane = lax.broadcasted_iota(jnp.int32, (SUB, LANES), 1)
    while len(parts) > 1:
        low = (lane & width) == 0
        merged = []
        for a, b in zip(parts[::2], parts[1::2]):
            merged.append(jnp.where(low, a, b) + pltpu.roll(jnp.where(low, b, a), width, 1))
        parts = merged
        width *= 2
    return parts[0]


def table_kernel(green_ref, inject_ref, rows1_ref, rows2_ref, out_ref, packed1_ref, packed2_ref, part_ref):
    slabs, _, states, columns = green_ref.shape
    chunks = columns // LANES
    groups = states // SUB
    for packed_ref, rows_ref in ((packed1_ref, rows1_ref), (packed2_ref, rows2_ref)):
        packed_ref[2 * slabs * SUB :] = rows_ref[...]
    for slab in range(slabs):
        weights = [
            [
                jnp.broadcast_to(inject_ref[slab, c : c + 1, k * LANES : (k + 1) * LANES], (SUB, LANES))
                for k in range(chunks)
            ]
            for c in range(2)
        ]

        def some_groups(i, _, slab=slab, weights=weights):
            for pair in range(PAIRS):
                sums = [[], []]
                for g in range(2):
                    rows = pl.ds(pl.multiple_of((i * (2 * PAIRS) + 2 * pair + g) * SUB, SUB), SUB)
                    total = [None, None]
                    for k in range(chunks):
                        cols = slice(k * LANES, (k + 1) * LANES)
                        re = green_ref[slab, 0, rows, cols]
                        im = green_ref[slab, 1, rows, cols]
                        squared = re * re + im * im
                        for c in range(2):
                            term = squared * weights[c][k]
                            total[c] = term if total[c] is None else total[c] + term
                    for c in range(2):
                        sums[c].append(total[c])
                for c in range(2):
                    part_ref[slab, c, i * PAIRS + pair] = merge(sums[c], 1)
            return _

        lax.fori_loop(0, groups // (2 * PAIRS), some_groups, None)
    lane = lax.broadcasted_iota(jnp.int32, (SUB, LANES), 1)
    count, width = groups // 2, 2
    while count > 1:
        low = (lane & width) == 0
        count //= 2
        for slab in range(slabs):
            for c in range(2):
                for k in range(count):
                    a, b = part_ref[slab, c, 2 * k], part_ref[slab, c, 2 * k + 1]
                    both = jnp.where(low, a, b) + pltpu.roll(jnp.where(low, b, a), width, 1)
                    if count > 1:
                        part_ref[slab, c, k] = both
                    else:
                        out_ref[slab, c] = both
                        at = (2 * slab + c) * SUB
                        packed1_ref[at : at + SUB] = both
                        packed2_ref[at : at + SUB] = both
        width *= 2


def orbital_table(green, inject, rows):
    slabs, _, states, _ = green.shape
    vmem = pl.BlockSpec(memory_space=pltpu.VMEM)
    packed = jax.ShapeDtypeStruct((2 * slabs * SUB + rows[0].shape[0], LANES), jnp.float32)
    return pl.pallas_call(
        table_kernel,
        in_specs=[vmem] * 4,
        out_specs=[vmem] * 3,
        out_shape=[jax.ShapeDtypeStruct((slabs, 2, SUB, LANES), jnp.float32), packed, packed],
        scratch_shapes=[pltpu.VMEM((slabs, 2, states // SUB // 2, SUB, LANES), jnp.float32)],
        compiler_params=pltpu.CompilerParams(vmem_limit_bytes=20 * MIB),
        cost_estimate=pl.CostEstimate(flops=0, bytes_accessed=TABLE_COST, transcendentals=0),
        name="table",
    )(green, inject, *rows)


def lookup(tables, choice):
    lane = choice >> 3
    group = choice & (SUB - 1)
    bits = [(group & (1 << b)) != 0 for b in range(3)]
    out = []
    for table in tables:
        found = [jnp.take_along_axis(t, lane, axis=1, mode="promise_in_bounds") for t in table]
        for bit in bits:
            found = [jnp.where(bit, found[2 * k + 1], found[2 * k]) for k in range(len(found) // 2)]
        out.append(found[0])
    return out


def permittivity(regions):
    return jnp.where(regions == 0, 1.0, jnp.where(regions == 1, 0.33, 1.7)).astype(jnp.float32)


def grouped(count, size, step, carry):
    odd = count % size
    if odd:
        carry = step(0, odd, carry)
    if count // size < 2:
        return step(odd, size, carry) if count >= size else carry
    return lax.fori_loop(0, count // size, lambda i, c: step(odd + i * size, size, c), carry)


def around(center, below, above, left, right):
    lane = lax.broadcasted_iota(jnp.int32, (SUB, LANES), 1)
    after = jnp.where(lane < LANES - 1, pltpu.roll(center, LANES - 1, 1), 0.0)
    ahead = jnp.where(lane > 0, pltpu.roll(center, 1, 1), 0.0)
    return above + below + right + left + after + ahead


def position():
    return lax.axis_index("energy"), lax.axis_index("space"), lax.axis_size("energy"), lax.axis_size("space")


NEAR = HALO - 1


def edge_kernel(
    regions_ref, dopant_ref, mesh_ref, old_ref, green_ref, inject_ref,
    rows1_ref, rows2_ref, planes1_ref, planes2_ref,
    regions_s, dopant_s, mesh_s, old_s, sems,
):
    e, s, ne, _ = position()
    odd_e, odd_s = (e & 1) == 1, (s & 1) == 1
    planes, own, _ = regions_s.shape
    pieces = [(regions_ref, regions_s), (dopant_ref, dopant_s)]
    for source, held in ((mesh_ref, mesh_s), (old_ref, old_s)):
        pieces.append((source.at[0:HALO], held.at[0]))
        pieces.append((source.at[planes - HALO : planes], held.at[1]))
    copies = [pltpu.make_async_copy(a, b, sems.at[k]) for k, (a, b) in enumerate(pieces)]
    for copy in copies:
        copy.start()
    for copy in copies[:2]:
        copy.wait()
    top, bottom = slice(0, NEAR), slice(own - NEAR, own)
    for p in range(planes):
        for field, values in ((0, permittivity(regions_s[p])), (1, dopant_s[p])):
            at = (field * planes + p) * NEAR
            rows1_ref[at : at + NEAR] = jnp.where(odd_e, values[top], values[bottom])
            rows2_ref[at : at + NEAR] = jnp.where(odd_e, values[bottom], values[top])
    for copy in copies[2:]:
        copy.wait()
    row0 = pl.multiple_of(e * own, SUB)
    up_from = pl.multiple_of(jnp.maximum(row0 - SUB, 0), SUB)
    down_from = pl.multiple_of(jnp.minimum(row0 + own, mesh_s.shape[2] - SUB), SUB)
    span = own + 2 * HALO
    for out_ref, side in ((planes1_ref, jnp.where(odd_s, 0, 1)), (planes2_ref, jnp.where(odd_s, 1, 0))):
        for k in range(NEAR):
            p, at = k + side, k * span
            out_ref[at : at + HALO] = mesh_s[side, p, pl.ds(up_from, SUB)][SUB - HALO :].astype(jnp.float32)
            out_ref[at + HALO : at + HALO + own] = mesh_s[side, p, pl.ds(row0, own)].astype(jnp.float32)
            out_ref[at + HALO + own : at + span] = mesh_s[side, p, pl.ds(down_from, SUB)][:HALO].astype(jnp.float32)
            low = planes - NEAR + k
            for field, at in ((0, (NEAR + HALO) * span + k * own), (1, (NEAR + HALO) * span + (NEAR + k) * own)):
                held = regions_s if field == 0 else dopant_s
                values = jnp.where(side == 0, held[k], held[low])
                out_ref[at : at + own] = permittivity(values) if field == 0 else values
        for k in range(HALO):
            at = (NEAR + k) * span
            out_ref[at : at + HALO] = jnp.where(e > 0, old_s[side, k, pl.ds(up_from, SUB)][SUB - HALO :], 0.0)
            out_ref[at + HALO : at + HALO + own] = old_s[side, k, pl.ds(row0, own)]
            out_ref[at + HALO + own : at + span] = jnp.where(
                e < ne - 1, old_s[side, k, pl.ds(down_from, SUB)][:HALO], 0.0
            )


def edges(regions, dopant, mesh, old, green, inject):
    planes, own, lanes = regions.shape
    rows = jax.ShapeDtypeStruct((2 * NEAR * planes, lanes), jnp.float32)
    cells = jax.ShapeDtypeStruct(((NEAR + HALO) * (own + 2 * HALO) + 2 * NEAR * own, lanes), jnp.float32)
    held = (2, HALO) + mesh.shape[1:]
    outs = pl.pallas_call(
        edge_kernel,
        in_specs=[pl.BlockSpec(memory_space=pl.ANY)] * 6,
        out_specs=[pl.BlockSpec(memory_space=pltpu.VMEM)] * 4,
        out_shape=[rows, rows, cells, cells],
        scratch_shapes=[
            pltpu.VMEM(regions.shape, jnp.int32),
            pltpu.VMEM(regions.shape, jnp.float32),
            pltpu.VMEM(held, jnp.int32),
            pltpu.VMEM(held, jnp.float32),
            pltpu.SemaphoreType.DMA((6,)),
        ],
        compiler_params=pltpu.CompilerParams(vmem_limit_bytes=8 * MIB),
        cost_estimate=pl.CostEstimate(flops=0, bytes_accessed=EDGE_COST, transcendentals=0),
        name="edges",
    )(*(pltpu.with_memory_space_constraint(x, pltpu.HBM) for x in (regions, dopant, mesh, old, green, inject)))
    return outs[:2], outs[2:]


def beside_rows(rows1_ref, rows2_ref, at):
    e, _, ne, _ = position()
    odd = (e & 1) == 1
    one = rows1_ref[at : at + NEAR]
    two = jnp.where((e > 0) & (e < ne - 1), rows2_ref[at : at + NEAR], 0.0)
    return jnp.where(odd, one, two), jnp.where(odd, two, one)


def join_kernel(*refs):
    rows1_ref, rows2_ref = refs[-5:-3]
    tables_ref, first_ref, second_ref = refs[-3:]
    odd_s = (lax.axis_index("space") & 1) == 1
    slabs = tables_ref.shape[0]
    ahead = 2 * slabs * SUB
    planes = (rows1_ref.shape[0] - ahead) // (2 * NEAR)
    tables = []
    for slab in range(slabs):
        for c in range(2):
            at = (2 * slab + c) * SUB
            terms = [ref[slab, c] if len(ref.shape) == 4 else ref[at : at + SUB] for ref in refs[:-5]]
            while len(terms) > 1:
                terms = [a + b for a, b in zip(terms[::2], terms[1::2])]
            tables_ref[slab, c] = terms[0]
            tables.append(terms[0])
    for k in range(NEAR):
        for field in range(2):
            low = beside_rows(rows1_ref, rows2_ref, ahead + (field * planes + k) * NEAR)
            high = beside_rows(rows1_ref, rows2_ref, ahead + (field * planes + planes - NEAR + k) * NEAR)
            top = (field * NEAR + k) * SUB
            for at, a, b in zip((top + 1, top + HALO), low, high):
                first_ref[at : at + NEAR] = jnp.where(odd_s, a, b)
                second_ref[at : at + NEAR] = jnp.where(odd_s, b, a)
    for c in range(2):
        top = (2 * NEAR + c) * SUB
        low, high = tables[c], tables[2 * (slabs - 1) + c]
        first_ref[top : top + SUB] = jnp.where(odd_s, low, high)
        second_ref[top : top + SUB] = jnp.where(odd_s, high, low)


def joined(terms, rows):
    vmem = pl.BlockSpec(memory_space=pltpu.VMEM)
    packed = jax.ShapeDtypeStruct((2 * (NEAR + 1) * SUB, LANES), jnp.float32)
    outs = pl.pallas_call(
        join_kernel,
        in_specs=[vmem] * (len(terms) + 2),
        out_specs=[vmem] * 3,
        out_shape=[jax.ShapeDtypeStruct(terms[0].shape, jnp.float32), packed, packed],
        compiler_params=pltpu.CompilerParams(vmem_limit_bytes=8 * MIB),
        name="join",
    )(*terms, *rows)
    return outs[0], outs[1:]


def broadcast_table(slab_value):
    return [[jnp.broadcast_to(slab_value[c, g : g + 1], (SUB, LANES)) for g in range(SUB)] for c in range(2)]


def first_sweep(choice, tables, center, bend, permit, dopant, outside):
    electrons, holes = lookup(tables, choice)
    if outside is not None:
        electrons, holes = jnp.where(outside, 1.0, electrons), jnp.where(outside, 1.0, holes)
    mismatch = permit * bend - (dopant + holes - electrons)
    jacobian = 6.0 * permit + electrons + holes
    return electrons, holes, center - mismatch / jacobian


def outside_rows(r, span):
    e, _, ne, _ = position()
    row = lax.broadcasted_iota(jnp.int32, (SUB, LANES), 0)
    outside = None
    if r == 0:
        outside = (row < HALO) & (e == 0)
    if r == span - SUB:
        below = (row >= SUB - HALO) & (e == ne - 1)
        outside = below if outside is None else outside | below
    return outside


def lay_kernel(mesh_ref, old_ref, planes1_ref, planes2_ref, mesh_x, before_x, bend_x):
    e, s, ne, _ = position()
    odd_s = (s & 1) == 1
    planes, span, _ = mesh_x.shape
    own = span - 2 * HALO
    row0 = pl.multiple_of(e * own, SUB)
    up, mid, down = slice(0, HALO), slice(HALO, HALO + own), slice(HALO + own, span)
    up_b, mid_b, down_b = (slice(PAD + x.start, PAD + x.stop) for x in (up, mid, down))
    up_from = pl.multiple_of(jnp.maximum(row0 - SUB, 0), SUB)
    down_from = pl.multiple_of(jnp.minimum(row0 + own, mesh_ref.shape[1] - SUB), SUB)

    def lay(first, count, _):
        for k in range(count):
            p = first + k
            q = p + HALO
            mesh_x[p, mid] = mesh_ref[p, pl.ds(row0, own)]
            mesh_x[p, up] = mesh_ref[p, pl.ds(up_from, SUB)][SUB - HALO :]
            mesh_x[p, down] = mesh_ref[p, pl.ds(down_from, SUB)][:HALO]
            before_x[q, mid_b] = old_ref[p, pl.ds(row0, own)]
            before_x[q, up_b] = jnp.where(e > 0, old_ref[p, pl.ds(up_from, SUB)][SUB - HALO :], 0.0)
            before_x[q, down_b] = jnp.where(e < ne - 1, old_ref[p, pl.ds(down_from, SUB)][:HALO], 0.0)
        return _

    grouped(planes, LAY, lay, None)
    for k in range(HALO):
        at = (NEAR + k) * span
        a, b = planes1_ref[at : at + span], planes2_ref[at : at + span]
        before_x[k, PAD : PAD + span] = jnp.where(odd_s, a, b)
        before_x[HALO + planes + k, PAD : PAD + span] = jnp.where(odd_s, b, a)

    def bends(first, count, _):
        for r in range(0, span, SUB):
            at = PAD + r
            held = [before_x[HALO + first + k, at : at + SUB] for k in range(-1, count + 1)]
            for k in range(count):
                q = HALO + first + k
                neighbours = around(
                    held[k + 1], held[k], held[k + 2],
                    before_x[q, at - 1 : at - 1 + SUB], before_x[q, at + 1 : at + 1 + SUB],
                )
                bend_x[first + k, r : r + SUB] = 6.0 * held[k + 1] - neighbours
        return _

    grouped(planes, BLOCK, bends, None)


def laid(mesh, old, beyond, own):
    planes, _, lanes = mesh.shape
    cells = (planes, own + 2 * HALO, lanes)
    padded = (planes + 2 * HALO, own + 2 * HALO + 2 * PAD, lanes)
    vmem = pl.BlockSpec(memory_space=pltpu.VMEM)
    f32 = jnp.float32
    return pl.pallas_call(
        lay_kernel,
        in_specs=[vmem] * 4,
        out_specs=[vmem] * 3,
        out_shape=[jax.ShapeDtypeStruct(*x) for x in ((cells, jnp.int32), (padded, f32), (cells, f32))],
        compiler_params=pltpu.CompilerParams(vmem_limit_bytes=16 * MIB),
        cost_estimate=pl.CostEstimate(flops=0, bytes_accessed=LAY_COST, transcendentals=0),
        name="lay",
    )(mesh, old, *beyond)


def later_sweep(center, below, above, left, right, before, permit, dopant, electrons, holes):
    moved = center - before
    electrons = electrons * jnp.exp(moved)
    holes = holes * jnp.exp(-moved)
    bend = 6.0 * center - around(center, below, above, left, right)
    mismatch = permit * bend - (dopant + holes - electrons)
    jacobian = 6.0 * permit + electrons + holes
    return center - mismatch / jacobian


def own_kernel(
    tables_ref, mesh_x, before_x, bend_x, regions_ref, dopant_ref, rows1_ref, rows2_ref,
    permit_x, dopant_x, electron_x, hole_x, change_x, most_x, *level_x,
):
    planes, own, _ = regions_ref.shape
    slabs = tables_ref.shape[0]
    span = own + 2 * HALO
    up, mid, down = slice(HALO - NEAR, HALO), slice(HALO, HALO + own), slice(HALO + own, HALO + own + NEAR)
    for p in range(planes):
        permit_x[p, mid] = permittivity(regions_ref[p])
        dopant_x[p, mid] = dopant_ref[p]
        for field, field_x in ((0, permit_x), (1, dopant_x)):
            at = 2 * slabs * SUB + (field * planes + p) * NEAR
            field_x[p, up], field_x[p, down] = beside_rows(rows1_ref, rows2_ref, at)
    for slab in range(slabs):
        tables = broadcast_table(tables_ref[slab])

        def some(first, count, _, tables=tables, slab=slab):
            for r in range(0, span, SUB):
                at, rows = PAD + r, slice(r, r + SUB)
                for k in range(count):
                    p = slab * PL + first + k
                    electron_x[p, rows], hole_x[p, rows], level_x[0][p, at : at + SUB] = first_sweep(
                        mesh_x[p, rows], tables, before_x[HALO + p, at : at + SUB], bend_x[p, rows],
                        permit_x[p, rows], dopant_x[p, rows], outside_rows(r, span),
                    )
            return _

        grouped(PL, LOOK, some, None)


    for sweep in range(1, SWEEPS):
        final = sweep == SWEEPS - 1
        starts = range(HALO, HALO + own, SUB) if final else range(0, span, SUB)

        def step(first, count, most, sweep=sweep, starts=starts, final=final):
            source = level_x[sweep - 1]
            for r in starts:
                rows = slice(r, r + SUB)
                at = PAD + r
                held = [source[sweep + first + k, at : at + SUB] for k in range(-1, count + 1)]
                for k in range(count):
                    p = sweep + first + k
                    before = before_x[HALO + p, at : at + SUB]
                    fresh = later_sweep(
                        held[k + 1], held[k], held[k + 2],
                        source[p, at - 1 : at - 1 + SUB], source[p, at + 1 : at + 1 + SUB],
                        before, permit_x[p, rows], dopant_x[p, rows], electron_x[p, rows], hole_x[p, rows],
                    )
                    if final:
                        change_x[p, r - HALO : r - HALO + SUB] = fresh - before
                        most = jnp.maximum(most, jnp.abs(fresh - before))
                    else:
                        level_x[sweep][p, at : at + SUB] = fresh
            return most

        most = grouped(planes - 2 * sweep, BLOCK, step, jnp.zeros((SUB, LANES), jnp.float32))
        if final:
            most_x[...] = most


def own_planes(tables, laid_out, regions, dopant, rows):
    vmem = pl.BlockSpec(memory_space=pltpu.VMEM)
    cells = laid_out[0].shape
    padded = (cells[0],) + laid_out[1].shape[1:]
    shapes = [cells] * 4 + [regions.shape, (SUB, LANES)] + [padded] * (SWEEPS - 1)
    return pl.pallas_call(
        own_kernel,
        in_specs=[vmem] * 8,
        out_specs=[vmem] * len(shapes),
        out_shape=[jax.ShapeDtypeStruct(shape, jnp.float32) for shape in shapes],
        compiler_params=pltpu.CompilerParams(vmem_limit_bytes=24 * MIB),
        cost_estimate=pl.CostEstimate(flops=0, bytes_accessed=LAY_COST, transcendentals=0),
        name="own",
    )(tables, *laid_out, regions, dopant, *rows)


def sweep_kernel(
    packed1_ref, packed2_ref, planes1_ref, planes2_ref, before_x, permit_o, dopant_o, electron_o, hole_o, change_o,
    most_o, level1_o, level2_o, level3_o, change_ref, most_ref, permit_s, dopant_s, electron_s, hole_s, level_s,
):
    _, s, _, ns = position()
    odd_s = (s & 1) == 1
    planes, own, _ = change_ref.shape
    span = own + 2 * HALO
    tops = range(0, span, SUB)
    levels_o = (level1_o, level2_o, level3_o)

    def plane_of(end, j):
        return j if end == 0 else planes + 2 * HALO - 1 - j

    for end in range(2):
        a, b = (packed1_ref, packed2_ref) if end == 0 else (packed2_ref, packed1_ref)
        c, d = (planes1_ref, planes2_ref) if end == 0 else (planes2_ref, planes1_ref)
        inside = s > 0 if end == 0 else s < ns - 1
        top = 2 * NEAR * SUB
        tables = [
            [
                jnp.where(
                    inside,
                    jnp.where(
                        odd_s,
                        jnp.broadcast_to(a[t + g : t + g + 1], (SUB, LANES)),
                        jnp.broadcast_to(b[t + g : t + g + 1], (SUB, LANES)),
                    ),
                    1.0,
                )
                for g in range(SUB)
            ]
            for t in (top, top + SUB)
        ]
        for j in range(1, HALO):
            q = plane_of(end, j)
            k = j - 1 if end == 0 else NEAR - j
            for field, field_s in ((0, permit_s), (1, dopant_s)):
                t = (field * NEAR + k) * SUB
                m = (NEAR + HALO) * span + (field * NEAR + k) * own
                field_s[end, j, :HALO] = jnp.where(odd_s, a[t : t + HALO], b[t : t + HALO])
                field_s[end, j, HALO : HALO + own] = jnp.where(odd_s, c[m : m + own], d[m : m + own])
                field_s[end, j, HALO + own :] = jnp.where(odd_s, a[t + HALO : t + SUB], b[t + HALO : t + SUB])
            for r in tops:
                at, rows = PAD + r, slice(r, r + SUB)
                here = slice(k * span + r, k * span + r + SUB)
                choice = jnp.where(odd_s, c[here], d[here]).astype(jnp.int32)
                center = before_x[q, at : at + SUB]
                neighbours = around(
                    center, before_x[q - 1, at : at + SUB], before_x[q + 1, at : at + SUB],
                    before_x[q, at - 1 : at - 1 + SUB], before_x[q, at + 1 : at + 1 + SUB],
                )
                electron_s[end, j, rows], hole_s[end, j, rows], level_s[end, 0, j, at : at + SUB] = first_sweep(
                    choice, tables, center, 6.0 * center - neighbours,
                    permit_s[end, j, rows], dopant_s[end, j, rows], outside_rows(r, span),
                )
        for sweep in range(1, SWEEPS):
            for j in (HALO + sweep - 1, HALO + sweep):
                p = plane_of(end, j) - HALO
                level_s[end, sweep - 1, j] = levels_o[sweep - 1][p]
    for p in range(SWEEPS - 1, planes - SWEEPS + 1):
        change_ref[p] = change_o[p]

    most = most_o[...]
    for sweep in range(1, SWEEPS):
        final = sweep == SWEEPS - 1
        for end in range(2):
            source = level_s.at[end, sweep - 1]
            for r in range(HALO, HALO + own, SUB) if final else tops:
                at, rows = PAD + r, slice(r, r + SUB)
                for j in range(1 + sweep, HALO + sweep):
                    q = plane_of(end, j)
                    p = q - HALO
                    if j < HALO:
                        fields = [ref[end, j, rows] for ref in (permit_s, dopant_s, electron_s, hole_s)]
                    else:
                        fields = [ref[p, rows] for ref in (permit_o, dopant_o, electron_o, hole_o)]
                    before = before_x[q, at : at + SUB]
                    fresh = later_sweep(
                        source[j, at : at + SUB], source[j - 1, at : at + SUB], source[j + 1, at : at + SUB],
                        source[j, at - 1 : at - 1 + SUB], source[j, at + 1 : at + 1 + SUB], before, *fields,
                    )
                    if final:
                        change_ref[p, r - HALO : r - HALO + SUB] = fresh - before
                        most = jnp.maximum(most, jnp.abs(fresh - before))
                    else:
                        level_s[end, sweep, j, at : at + SUB] = fresh
    most_ref[...] = jnp.broadcast_to(jnp.max(most, axis=0, keepdims=True)[None], most_ref.shape)


def swept(packed, beyond, fields, own):
    planes, span, lanes = fields[1].shape
    height = fields[0].shape[1]
    vmem = pl.BlockSpec(memory_space=pltpu.VMEM)
    f32 = jnp.float32
    return pl.pallas_call(
        sweep_kernel,
        in_specs=[vmem] * (4 + len(fields)),
        out_specs=[vmem, vmem],
        out_shape=[
            jax.ShapeDtypeStruct((planes, own, lanes), f32),
            jax.ShapeDtypeStruct((lax.axis_size(("energy", "space")), 1, lanes), f32),
        ],
        scratch_shapes=[pltpu.VMEM((2, HALO, span, lanes), f32)] * 4
        + [pltpu.VMEM((2, SWEEPS - 1, 2 * HALO, height, lanes), f32)],
        compiler_params=pltpu.CompilerParams(vmem_limit_bytes=24 * MIB),
        name="sweeps",
    )(*packed, *beyond, *fields)


def write_rows(out_ref, result, sems, old_ref, parts, masks, scale):
    e = lax.axis_index("energy")
    planes, own, _ = parts[0].shape
    size = planes // SETTLE
    copies = []
    for b in range(SETTLE):
        at = slice(b * size, (b + 1) * size)
        for k, (mask, part) in enumerate(zip(masks, parts)):
            rows = pl.ds(pl.multiple_of((e ^ mask) * own, SUB), own)
            result[k, at] = old_ref[at, rows] + part[at] * scale
            copies.append(pltpu.make_async_copy(result.at[k, at], out_ref.at[at, rows], sems.at[b, k]))
            copies[-1].start()
    for copy in copies:
        copy.wait()


def settle_kernel(most_ref, old_ref, *rest, masks):
    parts, (out_ref, scale_ref, result, sems) = rest[:-4], rest[-4:]
    scale = 1.0 / (1.0 + jnp.max(most_ref[...]))
    scale_ref[...] = jnp.full(scale_ref.shape, scale)
    write_rows(out_ref, result, sems, old_ref, parts, masks, scale)


def settle_more_kernel(scale_ref, old_ref, *rest, masks):
    parts, (_, out_ref, result, sems) = rest[:-4], rest[-4:]
    write_rows(out_ref, result, sems, old_ref, parts, masks, scale_ref[0:1][None])


def settled(most, old, parts, late):
    vmem, anywhere = pl.BlockSpec(memory_space=pltpu.VMEM), pl.BlockSpec(memory_space=pl.ANY)
    whole = jax.ShapeDtypeStruct(old.shape, jnp.float32)

    def scratch(count):
        return [
            pltpu.VMEM((count,) + parts[0].shape, jnp.float32),
            pltpu.SemaphoreType.DMA((SETTLE, count)),
        ]

    out, scale = pl.pallas_call(
        functools.partial(settle_kernel, masks=tuple(parts)),
        in_specs=[vmem] * (2 + len(parts)),
        out_specs=[anywhere, vmem],
        out_shape=[whole, jax.ShapeDtypeStruct((SUB, LANES), jnp.float32)],
        scratch_shapes=scratch(len(parts)),
        compiler_params=pltpu.CompilerParams(vmem_limit_bytes=16 * MIB),
        cost_estimate=pl.CostEstimate(flops=0, bytes_accessed=LAY_COST, transcendentals=0),
        name="settle",
    )(most, old, *parts.values())
    return pl.pallas_call(
        functools.partial(settle_more_kernel, masks=tuple(late)),
        in_specs=[vmem] * (2 + len(late)) + [anywhere],
        out_specs=anywhere,
        out_shape=whole,
        input_output_aliases={2 + len(late): 0},
        scratch_shapes=scratch(len(late)),
        compiler_params=pltpu.CompilerParams(vmem_limit_bytes=16 * MIB),
        name="settle_more",
    )(scale, old, *late.values(), out)


def pairs(axis, odd_first):
    count = lax.axis_size(axis)
    out = []
    for low in range(1 if odd_first else 0, count - 1, 2):
        out += [(low, low + 1), (low + 1, low)]
    return out


def toggled(x, axis, mask):
    return lax.ppermute(x, axis, [(i, i ^ mask) for i in range(lax.axis_size(axis))])


def on_device(green_blocks, injection, mesh_state_choice, regions, dopant_charge_field, earlier_voltage):
    ne = lax.axis_size("energy")
    own = regions.shape[1]
    green, inject = green_blocks[0], injection[0]

    def exchanged(sent, axis):
        return [lax.ppermute(x, axis, pairs(axis, odd_first)) for x, odd_first in zip(sent, (False, True))]

    rows, beyond = edges(regions, dopant_charge_field, mesh_state_choice, earlier_voltage, green, inject)
    beyond = exchanged(beyond, "space")
    tables, packed1, packed2 = orbital_table(green, inject, rows)
    packed1, beyond = lax.optimization_barrier((packed1, beyond))
    second = [k for k in range(3, ne) if k & (k + 1) == 0]
    terms = [tables]
    for k in range(1, ne):
        sent = packed1 if k == 1 else packed2 if k in second else tables
        terms.append(toggled(sent, "energy", k))
    e = lax.axis_index("energy")
    partner = jnp.where(e & 1 == 1, e + 1, e - 1)
    rows = [terms[1], terms[3]]
    for k in second[1:]:
        rows[1] = jnp.where(e ^ partner == k, terms[k], rows[1])
    laid_out = laid(mesh_state_choice, earlier_voltage, beyond, own)
    terms, laid_out = lax.optimization_barrier((terms, laid_out))
    tables, packed = joined(terms, rows)
    packed = exchanged(packed, "space")
    fields = own_planes(tables, laid_out, regions, dopant_charge_field, rows)
    change, most = swept(packed, beyond, (laid_out[1], *fields), own)
    parts, late = {0: change}, {}
    for k in range(2, ne, 2):
        parts[k] = toggled(change, "energy", k)
    parts[1] = toggled(change, "energy", 1)
    most = lax.all_to_all(most, ("energy", "space"), 0, 0)
    far = [parts[k] for k in range(2, ne, 2)]
    most, far = lax.optimization_barrier((most, far))
    for k, part in zip(range(2, ne, 2), far):
        late[k ^ 1] = toggled(part, "energy", 1)
    return settled(most, earlier_voltage, parts, late)


def solution(mesh):
    placed = (
        P("energy", "space", None, None, None),
        P("energy", "space", None, None),
        P("space", None, None),
        P("space", "energy", None),
        P("space", "energy", None),
        P("space", None, None),
    )
    return jax.shard_map(
        on_device, mesh=mesh, in_specs=placed, out_specs=P("space", None, None), check_vma=False
    )
```
